256 devices in a mesh: lat: 16 (over x_lo, y, core), lon: 16 (over z, x_hi).
Axes of the slice: x: 4 (x_hi: 2, x_lo: 2; x = x_hi * 2 + x_lo), y: 4, z: 8, core: 2. Of those that a mesh axis runs over, the one named last changes fastest.
Arguments:
- tokens: bfloat16 [128, 768, 512], P('lat', 'lon'), may hold values from -45 to 45
- region_ids: int32 [128, 768], P('lat', 'lon'), may hold values from 0 to 3
- bias_one: float32 [16, 64, 64], replicated, may hold values from -2 to 300
- qkv_one: bfloat16 [512, 1536], replicated, may hold values from -0.25 to 0.25
- out_one: bfloat16 [512, 512], replicated, may hold values from -0.25 to 0.25
- merge_proj: bfloat16 [2048, 1024], replicated, may hold values from -0.125 to 0.125
- bias_two: float32 [8, 64, 64], replicated, may hold values from -2 to 300
- qkv_two: bfloat16 [1024, 1536], replicated, may hold values from -0.1875 to 0.1875
- out_two: bfloat16 [512, 1024], replicated, may hold values from -0.25 to 0.25
Outputs:
- level_one: bfloat16 [128, 768, 512], P('lat', 'lon')
- level_two: bfloat16 [64, 384, 1024], P('lat', 'lon')
The draws below stay inside these ranges and needn't reach their ends.
All inputs are finite; a program needn't handle non-finite values.
Results may differ from the reference program's by a relative error of at most 0.0095.
Values may be sent and summed in bfloat16 or wider, within the bound.
No kernel may reach another device: no remote copies, remote signals or barrier semaphores. Data moves between devices by JAX's collectives and lax.ppermute only.
A program may use at most 192 MiB of HBM per device.

```python
import math
import jax
import jax.numpy as jnp
from jax import lax

D1 = 512
D2 = 1024
HEADS1 = 16
HD1 = 32
HEADS2 = 8
HD2 = 64
INNER2 = 512
WIN = 8
SHIFT = 4
NH = 128
NW = 768


def small_bias(key, head_count):
    side = WIN * WIN
    return jnp.clip(0.5 * jax.random.normal(key, (head_count, side, side), jnp.float32), -2.0, 2.0)


def draw_tokens(key, part):
    key = jax.random.fold_in(key, 11)
    base_key, row_key, col_key = jax.random.split(key, 3)
    low = math.log(0.3)
    high = math.log(3.0)
    row_scale = jnp.exp(jax.random.uniform(row_key, (NH, NW, 1), jnp.float32, low, high))
    col_scale = jnp.exp(jax.random.uniform(col_key, (D1,), jnp.float32, low, high))
    base = jnp.clip(jax.random.normal(base_key, (NH, NW, D1), jnp.float32), -5.0, 5.0)
    return (base * row_scale * col_scale).astype(jnp.bfloat16)


def draw_bias_one(key, part):
    key = jax.random.fold_in(key, 23)
    base_key = jax.random.fold_in(key, 0)
    table = small_bias(base_key, HEADS1)
    return table


def draw_bias_two(key, part):
    key = jax.random.fold_in(key, 37)
    base_key = jax.random.fold_in(key, 0)
    table = small_bias(base_key, HEADS2)
    return table


def touch_ends(entries, own_key, least, high):
    place = [jax.random.randint(jax.random.fold_in(own_key, axis), (), 0, length) for axis, length in enumerate(entries.shape)]
    widest = entries.shape.index(max(entries.shape))
    neighbour = place[:widest] + [(place[widest] + 1) % entries.shape[widest]] + place[widest + 1:]
    return entries.at[tuple(place)].set(least).at[tuple(neighbour)].set(high)


def bell_draw(own_key, extent, deviation, limit, kind=jnp.bfloat16):
    return jnp.clip(deviation * jax.random.normal(own_key, extent, jnp.float32), -limit, limit).astype(kind)


def setup_inputs(seed: int = 0) -> dict:
    keys = jax.random.split(jax.random.key(seed), 10)
    return {
        "tokens": draw_tokens(jax.random.fold_in(keys[9], 71), 0),
        "region_ids": touch_ends(jax.random.randint(keys[1], (NH, NW), 0, 4), jax.random.fold_in(keys[1], 1), 0, 3).astype(jnp.int32),
        "bias_one": draw_bias_one(jax.random.fold_in(keys[9], 71), 0),
        "qkv_one": bell_draw(keys[3], (D1, 3 * D1), D1 ** -0.5, 0.25),
        "out_one": bell_draw(keys[4], (D1, D1), D1 ** -0.5, 0.25),
        "merge_proj": bell_draw(keys[5], (4 * D1, D2), (4 * D1) ** -0.5, 0.125),
        "bias_two": draw_bias_two(jax.random.fold_in(keys[9], 71), 0),
        "qkv_two": bell_draw(keys[7], (D2, 3 * INNER2), D2 ** -0.5, 0.1875),
        "out_two": bell_draw(keys[8], (INNER2, D2), INNER2 ** -0.5, 0.25),
    }


EPSILON = 1e-05

def layer_norm(vectors):
    centered = vectors - lax.optimization_barrier(jnp.mean(vectors, axis=-1, keepdims=True))
    spread = lax.optimization_barrier(jnp.mean(centered * centered, axis=-1, keepdims=True))
    return centered * lax.rsqrt(spread + EPSILON)

def to_windows(source, window):
    num_rows, num_cols = (source.shape[0], source.shape[1])
    trailing = source.shape[2:]
    arranged = source.reshape((num_rows // window, window, num_cols // window, window) + trailing)
    arranged = jnp.swapaxes(arranged, 1, 2)
    return arranged.reshape((num_rows // window * (num_cols // window), window * window) + trailing)

def from_windows(source, num_rows, num_cols, window):
    trailing = source.shape[2:]
    arranged = source.reshape((num_rows // window, num_cols // window, window, window) + trailing)
    arranged = jnp.swapaxes(arranged, 1, 2)
    return arranged.reshape((num_rows, num_cols) + trailing)

def attend(queries, key_tiles, value_tiles, bias_table, allowed, head_dim):
    scores = jnp.einsum('wqhd,wkhd->whqk', queries.astype(jnp.float32), key_tiles.astype(jnp.float32))
    scores = scores / math.sqrt(head_dim) + bias_table[None].astype(jnp.float32)
    if allowed is not None:
        scores = jnp.where(allowed[:, None], scores, -1e+30)
    maximum = lax.optimization_barrier(jnp.max(scores, axis=-1, keepdims=True))
    weights = jnp.exp(scores - maximum)
    if allowed is not None:
        weights = jnp.where(allowed[:, None], weights, 0.0)
    probabilities = (weights / lax.optimization_barrier(jnp.sum(weights, axis=-1, keepdims=True))).astype(jnp.bfloat16)
    return jnp.einsum('whqk,wkhd->wqhd', probabilities.astype(jnp.float32), value_tiles.astype(jnp.float32)).astype(jnp.bfloat16)

def reference(tokens, region_ids, bias_one, qkv_one, out_one, merge_proj, bias_two, qkv_two, out_two):
    rolled = jnp.roll(tokens, (SHIFT, SHIFT), axis=(0, 1))
    rolled_ids = jnp.roll(region_ids, (SHIFT, SHIFT), axis=(0, 1))
    row_index = jnp.arange(NH, dtype=jnp.int32)
    band_ids = ((row_index - SHIFT) % NH + SHIFT) // WIN
    blocks = (rolled.reshape(NH // WIN, WIN, NW, D1), rolled_ids.reshape(NH // WIN, WIN, NW), band_ids.reshape(NH // WIN, WIN))

    def one_band(band_tiles):
        slab, slab_ids, slab_bands = band_tiles
        flattened = slab.reshape(-1, D1)
        normed = layer_norm(flattened.astype(jnp.float32)).astype(jnp.bfloat16)
        projected = jnp.dot(normed, qkv_one, preferred_element_type=jnp.float32).astype(jnp.bfloat16)
        windows = to_windows(projected.reshape(WIN, NW, 3 * D1), WIN)
        queries = windows[..., :D1].reshape(-1, WIN * WIN, HEADS1, HD1)
        key_tiles = windows[..., D1:2 * D1].reshape(-1, WIN * WIN, HEADS1, HD1)
        value_tiles = windows[..., 2 * D1:].reshape(-1, WIN * WIN, HEADS1, HD1)
        id_tiles = to_windows(slab_ids, WIN)
        band_tiles_win = to_windows(jnp.broadcast_to(slab_bands[:, None], (WIN, NW)), WIN)
        allowed = (id_tiles[:, :, None] == id_tiles[:, None, :]) & (band_tiles_win[:, :, None] == band_tiles_win[:, None, :])
        attended = attend(queries, key_tiles, value_tiles, bias_one, allowed, HD1).reshape(-1, WIN * WIN, D1)
        attended = from_windows(attended, WIN, NW, WIN).reshape(-1, D1)
        updated = flattened.astype(jnp.float32) + jnp.dot(attended, out_one, preferred_element_type=jnp.float32)
        return updated.astype(jnp.bfloat16).reshape(WIN, NW, D1)
    out_rolled = lax.map(one_band, blocks).reshape(NH, NW, D1)
    level_one = jnp.roll(out_rolled, (-SHIFT, -SHIFT), axis=(0, 1))
    double_bands = level_one.reshape(NH // (2 * WIN), 2 * WIN, NW, D1)

    def level_two_band(band_tiles):
        quartet = jnp.concatenate([band_tiles[0::2, 0::2], band_tiles[1::2, 0::2], band_tiles[0::2, 1::2], band_tiles[1::2, 1::2]], axis=-1)
        normed = layer_norm(quartet.astype(jnp.float32)).astype(jnp.bfloat16).reshape(-1, 4 * D1)
        merged = jnp.dot(normed, merge_proj, preferred_element_type=jnp.float32).astype(jnp.bfloat16)
        normed_two = layer_norm(merged.astype(jnp.float32)).astype(jnp.bfloat16)
        projected = jnp.dot(normed_two, qkv_two, preferred_element_type=jnp.float32).astype(jnp.bfloat16)
        windows = to_windows(projected.reshape(WIN, NW // 2, 3 * INNER2), WIN)
        queries = windows[..., :INNER2].reshape(-1, WIN * WIN, HEADS2, HD2)
        key_tiles = windows[..., INNER2:2 * INNER2].reshape(-1, WIN * WIN, HEADS2, HD2)
        value_tiles = windows[..., 2 * INNER2:].reshape(-1, WIN * WIN, HEADS2, HD2)
        attended = attend(queries, key_tiles, value_tiles, bias_two, None, HD2).reshape(-1, WIN * WIN, INNER2)
        attended = from_windows(attended, WIN, NW // 2, WIN).reshape(-1, INNER2)
        updated = merged.astype(jnp.float32) + jnp.dot(attended, out_two, preferred_element_type=jnp.float32)
        return updated.astype(jnp.bfloat16).reshape(WIN, NW // 2, D2)
    level_two = lax.map(level_two_band, double_bands).reshape(NH // 2, NW // 2, D2)
    return (level_one, level_two)
```

```python
import math

import jax
import jax.numpy as jnp
from jax import lax
from jax.experimental import pallas as pl
from jax.experimental.pallas import tpu as pltpu
from jax.sharding import PartitionSpec as P

EPSILON = 1e-05
LOG2E = math.log2(math.e)
BF = jnp.bfloat16
F32 = jnp.float32
ROWS = 8
COLS = 48
TILES = 7
FRAME = 56
D1 = 512
D2 = 1024
VMEM_BYTES = 44 * 1024 * 1024

NT = (((1,), (1,)), ((), ()))
TN = (((0,), (0,)), ((), ()))


def params():
    return pltpu.CompilerParams(vmem_limit_bytes=VMEM_BYTES)


def layer_norm(x):
    width = x.shape[-1]
    mean = jnp.sum(x, axis=-1, keepdims=True) * (1.0 / width)
    c = x - mean
    var = jnp.sum(c * c, axis=-1, keepdims=True) * (1.0 / width)
    return c * lax.rsqrt(var + EPSILON)


def id_rows(ids_ref):
    ids = ids_ref[...].astype(F32)
    return jnp.concatenate([ids, jnp.zeros((ROWS, 128 - COLS), F32)], axis=1)


def edge_kernel(tok_ref, ids_ref, east_ref, west_ref):
    last, first = [], []
    for r in range(ROWS):
        last.append(tok_ref[r, 32:48, :].astype(F32)[12:16])
        first.append(tok_ref[r, 0:16, :].astype(F32)[0:4])
    ids = id_rows(ids_ref)
    wide = jnp.concatenate([ids, jnp.zeros((ROWS, D1 - 128), F32)], axis=1)
    rolled = jnp.concatenate(
        [pltpu.roll(ids, 128 - (COLS - 4), 1), jnp.zeros((ROWS, D1 - 128), F32)], axis=1
    )
    pad = jnp.zeros((ROWS, D1), F32)
    east_ref[...] = jnp.concatenate(last + [rolled, pad], axis=0).astype(BF)
    west_ref[...] = jnp.concatenate(first + [wide, pad], axis=0).astype(BF)


def framed_row(tok_ref, west_ref, east_ref, r):
    start = (r // 4) * 16
    w = west_ref[start : start + 16, :].astype(F32)[(r % 4) * 4 : (r % 4) * 4 + 4]
    e = east_ref[start : start + 16, :].astype(F32)[(r % 4) * 4 : (r % 4) * 4 + 4]
    return jnp.concatenate([w, tok_ref[r].astype(F32), e], axis=0)


def framed_ids(ids_ref, west_ref, east_ref):
    lane = lax.broadcasted_iota(jnp.int32, (ROWS, 128), 1)
    own = pltpu.roll(id_rows(ids_ref), 4, 1)
    w = west_ref[32:48, 0:128].astype(F32)[0:8]
    e = pltpu.roll(east_ref[32:48, 0:128].astype(F32)[0:8], COLS + 4, 1)
    return jnp.where(lane < 4, w, jnp.where(lane < COLS + 4, own, e))


def band_kernel(tok_ref, ids_ref, west_ref, east_ref, cross_ref, pair_ref):
    ids = framed_ids(ids_ref, west_ref, east_ref)
    parity = lax.rem(lax.axis_index("lat"), 2)
    halves = []
    for h in range(2):
        rows = [framed_row(tok_ref, west_ref, east_ref, 4 * h + r) for r in range(4)]
        id_part = ids if h == 0 else pltpu.roll(ids, 4, 0)
        id_part = jnp.concatenate([id_part, jnp.zeros((ROWS, D1 - 128), F32)], axis=1)
        rows += [id_part, jnp.zeros((ROWS, D1), F32)]
        halves.append(jnp.concatenate(rows, axis=0).astype(BF))

    @pl.when(parity == 0)
    def _():
        cross_ref[...] = halves[0]
        pair_ref[...] = halves[1]

    @pl.when(parity == 1)
    def _():
        cross_ref[...] = halves[1]
        pair_ref[...] = halves[0]


def bias_kernel(one_ref, two_ref, one_out, two_out):
    for half in range(2):
        low = 32 * (1 - half)
        for g in range(4):
            part = one_ref[4 * g : 4 * g + 4, low : low + 32, :].reshape(128, 64)
            one_out[half, g] = part.T * LOG2E
    parity = lax.rem(lax.axis_index("lat"), 2)
    low = pl.multiple_of(parity * 32, 32)
    for g in range(2):
        part = two_ref[4 * g : 4 * g + 4, pl.ds(low, 32), :].reshape(128, 64)
        two_out[g] = part.T * LOG2E


def masked_heads(q, head_dim, count):
    lane = lax.broadcasted_iota(jnp.int32, q.shape, 1) // head_dim
    zero = jnp.zeros_like(q)
    return jnp.concatenate([jnp.where(lane == h, q, zero) for h in range(count)], axis=0)


def pick_heads(o, head_dim, count):
    rows = o.shape[0] // count
    lane = lax.broadcasted_iota(jnp.int32, (rows, o.shape[1]), 1) // head_dim
    out = o[0:rows]
    for h in range(1, count):
        out = jnp.where(lane == h, o[h * rows : (h + 1) * rows], out)
    return out


def softmax_keys(s, allowed):
    if allowed is not None:
        s = jnp.where(allowed, s, -1e30)
    p = jnp.exp2(s - jnp.max(s, axis=0, keepdims=True))
    return p * (1.0 / jnp.sum(p, axis=0, keepdims=True))


def main_kernel(
    tok_ref, ids_ref, west_ref, east_ref, cross_ref, pair_ref, bias_ref, qkv_ref,
    out_hbm, merge_hbm, two_hbm,
    one_out, merged_out, query_out, kv_out,
    normed, hot, kv, query, attended, projected, level, parts, out_w, merge_w, two_w, sems,
):
    loads = [
        pltpu.make_async_copy(out_hbm, out_w, sems.at[0]),
        pltpu.make_async_copy(merge_hbm, merge_w, sems.at[1]),
        pltpu.make_async_copy(two_hbm, two_w, sems.at[2]),
    ]
    for load in loads:
        load.start()
    lat = lax.axis_index("lat")
    last = lax.axis_size("lat") - 1
    parity = lax.rem(lat, 2)

    def halo_ids(ref):
        return ref[224:240, 0:128].astype(F32)[0:8]

    cross_ids, pair_ids = halo_ids(cross_ref), halo_ids(pair_ref)
    above = jnp.where(parity == 0, cross_ids, pair_ids)
    below = jnp.where(parity == 0, pair_ids, cross_ids)
    above = jnp.where(lat == 0, -1.0, above)
    below = jnp.where(lat == last, -1.0, below)
    own = framed_ids(ids_ref, west_ref, east_ref)
    frame = jnp.concatenate([above[0:4], own, below[0:4]], axis=0)
    frame = jnp.concatenate([frame, jnp.zeros((112, 128), F32)], axis=0)
    turned = frame.T
    lane = lax.broadcasted_iota(jnp.int32, (FRAME, 128), 1).astype(F32)
    for half in range(2):
        for r in range(0, ROWS, 2):
            pair = []
            for k in range(2):
                at = half * 8 + r + k
                col = jnp.broadcast_to(turned[0:FRAME, at : at + 1], (FRAME, 128))
                pair.append(jnp.where(col == lane, 1.0, 0.0).reshape(TILES, 8, 128))
            hot[half, :, r // 2] = jnp.concatenate(pair, axis=1).astype(BF)

    def put(half, r, rows):
        pair = [layer_norm(x).reshape(TILES, 8, D1) for x in rows]
        normed[half, :, r // 2] = jnp.concatenate(pair, axis=1).astype(BF)

    for r in range(0, ROWS, 2):
        rows = [framed_row(tok_ref, west_ref, east_ref, r + k) for k in range(2)]
        put(r // 4, (r + 4) % 8, rows)
    for r in range(0, 4, 2):
        block = slice(r * FRAME, (r + 2) * FRAME)
        c = cross_ref[block, :].astype(F32)
        p = pair_ref[block, :].astype(F32)
        a = jnp.where(parity == 0, c, p)
        b = jnp.where(parity == 0, p, c)
        put(0, r, [a[0:FRAME], a[FRAME:]])
        put(1, 4 + r, [b[0:FRAME], b[FRAME:]])

    for half in range(2):
        x = normed[half].reshape(TILES * 64, D1)
        kv[half] = jnp.dot(x, qkv_ref[:, D1:], preferred_element_type=F32).astype(BF).reshape(
            TILES, 64, 2 * D1
        )
        low = 2 * (1 - half)
        x = normed[half, :, low : low + 2].reshape(TILES * 32, D1)
        query[half] = jnp.dot(x, qkv_ref[:, :D1], preferred_element_type=F32).astype(BF).reshape(
            TILES, 32, D1
        )

    scale = LOG2E / math.sqrt(32)

    def window(j, carry):
        for half in range(2):
            keys_hot = hot[half, j].reshape(64, 128)
            low = 32 * (1 - half)
            q_hot = keys_hot[low : low + 32]
            same = lax.dot_general(
                keys_hot, jnp.concatenate([q_hot] * 4, axis=0), NT, preferred_element_type=F32
            )
            allowed = same > 0.5
            for g in range(4):
                lanes = slice(g * 128, g * 128 + 128)
                v_lanes = slice(D1 + g * 128, D1 + g * 128 + 128)
                q = masked_heads(query[half, j, :, lanes], 32, 4)
                s = lax.dot_general(kv[half, j, :, lanes], q, NT, preferred_element_type=F32)
                p = softmax_keys(s * scale + bias_ref[half, g], allowed)
                o = lax.dot_general(
                    p.astype(BF), kv[half, j, :, v_lanes], TN, preferred_element_type=F32
                )
                attended[half, j, :, lanes] = pick_heads(o, 32, 4).astype(BF)
        return carry

    lax.fori_loop(0, TILES, window, 0)

    loads[0].wait()
    for half in range(2):
        x = attended[half].reshape(TILES * 32, D1)
        projected[half] = jnp.dot(x, out_w[...], preferred_element_type=F32).reshape(
            TILES, 4, 8, D1
        )
    for r in range(ROWS):
        add = projected[r // 4, :, r % 4].reshape(FRAME, D1)[4 : 4 + COLS]
        done = (tok_ref[r].astype(F32) + add).astype(BF)
        one_out[r] = done
        for n in range(4):
            level[n, r] = done[:, n * 128 : n * 128 + 128].astype(F32)

    for i in range(4):
        quartet = [
            jnp.concatenate(
                [level[n, 2 * i + dr, pl.ds(dc, COLS // 2, 2), :] for n in range(4)], axis=1
            )
            for dc in range(2)
            for dr in range(2)
        ]
        total = sum(jnp.sum(x, axis=-1, keepdims=True) for x in quartet)
        quartet = [x - total * (1.0 / (4 * D1)) for x in quartet]
        total = sum(jnp.sum(x * x, axis=-1, keepdims=True) for x in quartet)
        factor = lax.rsqrt(total * (1.0 / (4 * D1)) + EPSILON)
        for n in range(4):
            parts[n, :, i] = (quartet[n] * factor).reshape(3, 8, D1)
    loads[1].wait()
    merged = jnp.zeros((96, D2), F32)
    for n in range(4):
        merged += jnp.dot(
            parts[n].reshape(96, D1).astype(BF),
            merge_w[n * D1 : (n + 1) * D1, :],
            preferred_element_type=F32,
        )
    merged = merged.astype(BF)
    merged_out[...] = merged
    x = layer_norm(merged.astype(F32)).astype(BF)
    loads[2].wait()
    kv_out[...] = jnp.dot(x, two_w[:, 512:], preferred_element_type=F32).astype(BF)
    query_out[...] = jnp.dot(x, two_w[:, :512], preferred_element_type=F32).astype(BF)


def level_two_kernel(
    query_ref, kv_ref, other_ref, merged_ref, bias_ref, out_ref, two_out, keys, attended, result
):
    parity = lax.rem(lax.axis_index("lat"), 2)
    mine = pl.multiple_of(parity * 32, 32)
    theirs = pl.multiple_of(32 - parity * 32, 32)
    scale = LOG2E / math.sqrt(64)
    for w in range(3):
        keys[w, pl.ds(mine, 32), :] = kv_ref[w * 32 : w * 32 + 32, :]
        keys[w, pl.ds(theirs, 32), :] = other_ref[w * 32 : w * 32 + 32, :]
    for w in range(3):
        for g in range(2):
            lanes = slice(g * 256, g * 256 + 256)
            v_lanes = slice(512 + g * 256, 512 + g * 256 + 256)
            q = masked_heads(query_ref[w * 32 : w * 32 + 32, lanes], 64, 4)
            s = lax.dot_general(keys[w, :, lanes], q, NT, preferred_element_type=F32)
            p = softmax_keys(s * scale + bias_ref[g], None)
            o = lax.dot_general(p.astype(BF), keys[w, :, v_lanes], TN, preferred_element_type=F32)
            attended[w * 32 : w * 32 + 32, lanes] = pick_heads(o, 64, 4).astype(BF)
    add = jnp.dot(attended[...], out_ref[...], preferred_element_type=F32)
    result[...] = (merged_ref[...].astype(F32) + add).reshape(3, 4, 8, D2)
    for i in range(4):
        two_out[i] = result[:, i].reshape(24, D2).astype(BF)


def vmem(count):
    return [pl.BlockSpec(memory_space=pltpu.VMEM)] * count


def call(kernel, outs, args, hbm=0, scratch=(), flops=1000, size=1000):
    shapes = [jax.ShapeDtypeStruct(s, d) for s, d in outs]
    return pl.pallas_call(
        kernel,
        out_shape=shapes,
        in_specs=vmem(len(args) - hbm) + [pl.BlockSpec(memory_space=pl.ANY)] * hbm,
        out_specs=vmem(len(outs)),
        scratch_shapes=list(scratch),
        compiler_params=params(),
        cost_estimate=pl.CostEstimate(flops=flops, bytes_accessed=size, transcendentals=0),
    )(*args)


def on_device(
    tokens, region_ids, bias_one, qkv_one, out_one, merge_proj, bias_two, qkv_two, out_two
):
    lat_count = lax.axis_size("lat")
    lon_count = lax.axis_size("lon")
    pairs = [(i, i ^ 1) for i in range(lat_count)]
    across = [(i, (i + (1 if i % 2 else -1)) % lat_count) for i in range(lat_count)]
    eastward = [(i, (i + 1) % lon_count) for i in range(lon_count)]
    westward = [(i, (i - 1) % lon_count) for i in range(lon_count)]

    to_east, to_west = call(edge_kernel, [((48, D1), BF)] * 2, [tokens, region_ids])
    from_west = lax.ppermute(to_east, "lon", eastward)
    from_east = lax.ppermute(to_west, "lon", westward)
    table_one, table_two = call(
        bias_kernel, [((2, 4, 64, 128), F32), ((2, 64, 128), F32)], [bias_one, bias_two],
        flops=10**9, size=10**6,
    )
    to_cross, to_pair = call(
        band_kernel, [((240, D1), BF)] * 2, [tokens, region_ids, from_west, from_east]
    )
    from_cross = lax.ppermute(to_cross, "lat", across)
    from_pair = lax.ppermute(to_pair, "lat", pairs)
    level_one, merged, query, kv = call(
        main_kernel,
        [((ROWS, COLS, D1), BF), ((96, D2), BF), ((96, 512), BF), ((96, 1024), BF)],
        [
            tokens, region_ids, from_west, from_east, from_cross, from_pair, table_one, qkv_one,
            out_one, merge_proj, qkv_two,
        ],
        hbm=3,
        scratch=[
            pltpu.VMEM((2, TILES, 4, 16, D1), BF),
            pltpu.VMEM((2, TILES, 4, 16, 128), BF),
            pltpu.VMEM((2, TILES, 64, 2 * D1), BF),
            pltpu.VMEM((2, TILES, 32, D1), BF),
            pltpu.VMEM((2, TILES, 32, D1), BF),
            pltpu.VMEM((2, TILES, 4, 8, D1), F32),
            pltpu.VMEM((4, ROWS, COLS, 128), F32),
            pltpu.VMEM((4, 3, 4, 8, D1), F32),
            pltpu.VMEM((D1, D1), BF),
            pltpu.VMEM((4 * D1, D2), BF),
            pltpu.VMEM((D2, 1536), BF),
            pltpu.SemaphoreType.DMA((3,)),
        ],
        flops=3 * 10**9, size=10**7,
    )
    other = lax.ppermute(kv, "lat", pairs)
    (level_two,) = call(
        level_two_kernel,
        [((4, 24, D2), BF)],
        [query, kv, other, merged, table_two, out_two],
        scratch=[
            pltpu.VMEM((3, 64, 1024), BF),
            pltpu.VMEM((96, 512), BF),
            pltpu.VMEM((3, 4, 8, D2), F32),
        ],
        flops=10**9, size=10**6,
    )
    return (level_one, level_two)


def solution(mesh):
    placed = (P("lat", "lon", None), P("lat", "lon"), P(), P(), P(), P(), P(), P(), P())
    return jax.shard_map(
        on_device,
        mesh=mesh,
        in_specs=placed,
        out_specs=(P("lat", "lon", None), P("lat", "lon", None)),
        check_vma=False,
    )
```

```python
import math

import jax
import jax.numpy as jnp
from jax import lax
from jax.experimental import pallas as pl
from jax.experimental.pallas import tpu as pltpu
from jax.sharding import PartitionSpec as P

EPSILON = 1e-05
LOG2E = math.log2(math.e)
BF = jnp.bfloat16
F32 = jnp.float32
ROWS = 8
COLS = 48
TILES = 7
INSIDE = 5
FRAME = 56
D1 = 512
D2 = 1024
MIB = 1024 * 1024

NT = (((1,), (1,)), ((), ()))
TN = (((0,), (0,)), ((), ()))


def layer_norm(x):
    width = x.shape[-1]
    mean = jnp.sum(x, axis=-1, keepdims=True) * (1.0 / width)
    c = x - mean
    var = jnp.sum(c * c, axis=-1, keepdims=True) * (1.0 / width)
    return c * lax.rsqrt(var + EPSILON)


def lanes_to(x, width):
    return jnp.concatenate([x, jnp.zeros((x.shape[0], width - x.shape[1]), x.dtype)], axis=1)


def lat_parity():
    return lax.rem(lax.axis_index("lat"), 2)


def lon_parity():
    return lax.rem(lax.axis_index("lon"), 2)


def start_all(pairs, sems):
    copies = [pltpu.make_async_copy(src, dst, sems.at[n]) for n, (src, dst) in enumerate(pairs)]
    for copy in copies:
        copy.start()
    return copies


def edge_kernel(tok_hbm, ids_hbm, inner_ref, outer_ref, tok_ref, ids_ref, sems):
    copies = start_all(
        [
            (ids_hbm, ids_ref),
            (tok_hbm.at[:, 0:16], tok_ref.at[:, 0:16]),
            (tok_hbm.at[:, 32:48], tok_ref.at[:, 32:48]),
            (tok_hbm.at[:, 16:32], tok_ref.at[:, 16:32]),
        ],
        sems,
    )
    for copy in copies[:3]:
        copy.wait()
    first = [tok_ref[r, 0:16].astype(F32)[0:4] for r in range(ROWS)]
    last = [tok_ref[r, 32:48].astype(F32)[12:16] for r in range(ROWS)]
    ids = lanes_to(ids_ref[...].astype(F32), 128)
    pad = jnp.zeros((ROWS, D1), F32)
    first = jnp.concatenate(first + [lanes_to(ids, D1), pad], axis=0).astype(BF)
    ids = pltpu.roll(ids, 128 - (COLS - 4), 1)
    last = jnp.concatenate(last + [lanes_to(ids, D1), pad], axis=0).astype(BF)
    even = lon_parity() == 0
    inner_ref[...] = jnp.where(even, last, first)
    outer_ref[...] = jnp.where(even, first, last)
    copies[3].wait()


def sides(inner_ref, outer_ref):
    inner, outer = inner_ref[...].astype(F32), outer_ref[...].astype(F32)
    even = lon_parity() == 0
    return jnp.where(even, outer, inner), jnp.where(even, inner, outer)


def own_kernel(
    qkv_hbm, one_hbm, two_hbm, out_hbm, next_hbm, tok_ref,
    inside_out, one_out, two_out, qkv_ref, out_ref, next_ref,
    normed, one_ref, two_ref, sems,
):
    copies = start_all(
        [
            (one_hbm, one_ref),
            (two_hbm, two_ref),
            (qkv_hbm, qkv_ref),
            (out_hbm, out_ref),
            (next_hbm, next_ref),
        ],
        sems,
    )
    for r in range(0, ROWS, 2):
        pair = []
        for k in range(2):
            x = layer_norm(tok_ref[r + k].astype(F32))
            pair.append(x[4 : COLS - 4].reshape(INSIDE, 8, D1))
        normed[r // 4, :, (r % 4) // 2] = jnp.concatenate(pair, axis=1).astype(BF)
    copies[0].wait()
    copies[1].wait()
    for half in range(2):
        low = 32 * (1 - half)
        for g in range(4):
            turned = one_ref[4 * g : 4 * g + 4, low : low + 32, :].reshape(128, 64).T * LOG2E
            one_out[half, g, 0:32] = turned[low : low + 32]
            one_out[half, g, 32:64] = turned[32 - low : 64 - low]
    low = pl.multiple_of(lat_parity() * 32, 32)
    for g in range(2):
        part = two_ref[4 * g : 4 * g + 4, pl.ds(low, 32), :].reshape(128, 64)
        two_out[g] = part.T * LOG2E
    copies[2].wait()
    x = normed[...].reshape(2 * INSIDE * 32, D1)
    inside_out[...] = (
        jnp.dot(x, qkv_ref[...], preferred_element_type=F32)
        .astype(BF)
        .reshape(2, INSIDE, 32, 3 * D1)
    )
    copies[3].wait()
    copies[4].wait()


def band_kernel(
    tok_ref, ids_ref, inner_ref, outer_ref, after_ref, cross_ref, pair_ref, frame_ref
):
    west, east = sides(inner_ref, outer_ref)
    lane = lax.broadcasted_iota(jnp.int32, (ROWS, 128), 1)
    own = pltpu.roll(lanes_to(ids_ref[...].astype(F32), 128), 4, 1)
    far = pltpu.roll(east[32:40, 0:128], COLS + 4, 1)
    ids = jnp.where(lane < 4, west[32:40, 0:128], jnp.where(lane < COLS + 4, own, far))
    frame_ref[...] = ids
    halves = []
    for h in range(2):
        rows = []
        for r in range(4 * h, 4 * h + 4):
            rows += [west[4 * r : 4 * r + 4], tok_ref[r].astype(F32), east[4 * r : 4 * r + 4]]
        rows.append(lanes_to(ids if h == 0 else pltpu.roll(ids, 4, 0), D1))
        rows.append(jnp.zeros((ROWS, D1), F32))
        halves.append(jnp.concatenate(rows, axis=0).astype(BF))
    even = lat_parity() == 0
    cross_ref[...] = jnp.where(even, halves[0], halves[1])
    pair_ref[...] = jnp.where(even, halves[1], halves[0])


def side_kernel(
    merge_hbm, last_hbm, tok_ref, inner_ref, outer_ref, qkv_ref, after_ref,
    qkv_out, merge_ref, last_ref, sems,
):
    copies = start_all([(merge_hbm, merge_ref), (last_hbm, last_ref)], sems)
    west, east = sides(inner_ref, outer_ref)
    rows = []
    for half in range(2):
        for r in range(4 * half, 4 * half + 4):
            rows += [west[4 * r : 4 * r + 4], tok_ref[r, 0:16].astype(F32)[0:4]]
        for r in range(4 * half, 4 * half + 4):
            rows += [tok_ref[r, 32:48].astype(F32)[12:16], east[4 * r : 4 * r + 4]]
    x = layer_norm(jnp.concatenate(rows, axis=0)).astype(BF)
    qkv_out[...] = (
        jnp.dot(x, qkv_ref[...], preferred_element_type=F32).astype(BF).reshape(2, 2, 32, 3 * D1)
    )
    for copy in copies:
        copy.wait()


def masked_heads(q, head_dim, count):
    lane = lax.broadcasted_iota(jnp.int32, q.shape, 1) // head_dim
    zero = jnp.zeros_like(q)
    return jnp.concatenate([jnp.where(lane == h, q, zero) for h in range(count)], axis=0)


def pick_heads(o, head_dim, count):
    rows = o.shape[0] // count
    lane = lax.broadcasted_iota(jnp.int32, (rows, o.shape[1]), 1) // head_dim
    out = o[0:rows]
    for h in range(1, count):
        out = jnp.where(lane == h, o[h * rows : (h + 1) * rows], out)
    return out


def softmax_keys(s, allowed):
    if allowed is not None:
        s = jnp.where(allowed, s, -1e30)
    p = jnp.exp2(s - jnp.max(s, axis=0, keepdims=True))
    return p * (1.0 / jnp.sum(p, axis=0, keepdims=True))


def half_attend(half, halo_ref, frame_ref, inside_ref, side_ref, qkv_ref, bias_ref, outside, normed):
    ids = frame_ref[...]
    own = jnp.where(half == 0, ids, pltpu.roll(ids, 4, 0))
    halo = jnp.where(outside, -1.0, halo_ref[224:240, 0:128].astype(F32)[0:8])
    frame = jnp.concatenate([own[0:4], halo[0:4], jnp.zeros((120, 128), F32)], axis=0)
    turned = frame.T
    lane = lax.broadcasted_iota(jnp.int32, (FRAME, 128), 1).astype(F32)
    hot = []
    for r in range(8):
        col = jnp.broadcast_to(turned[0:FRAME, r : r + 1], (FRAME, 128))
        hot.append(jnp.where(col == lane, 1.0, 0.0))

    def tile_of(rows, j):
        return jnp.concatenate([x[8 * j : 8 * j + 8] for x in rows], axis=0)

    for r in range(0, 4, 2):
        x = layer_norm(halo_ref[r * FRAME : (r + 2) * FRAME, :].astype(F32))
        pair = [x[k * FRAME : (k + 1) * FRAME].reshape(TILES, 8, D1) for k in range(2)]
        normed[:, r // 2] = jnp.concatenate(pair, axis=1).astype(BF)
    halo_kv = jnp.dot(
        normed[...].reshape(TILES * 32, D1), qkv_ref[:, D1:], preferred_element_type=F32
    ).astype(BF)

    scale = LOG2E / math.sqrt(32)
    units = [(j, g) for j in range(TILES) for g in range(4)]

    def own_part(j, block, g):
        lanes = slice(block * D1 + g * 128, block * D1 + g * 128 + 128)
        if 0 < j < TILES - 1:
            return inside_ref[half, j - 1, :, lanes]
        return side_ref[half, j // (TILES - 1), :, lanes]

    def both(j, block, g):
        lanes = slice((block - 1) * D1 + g * 128, (block - 1) * D1 + g * 128 + 128)
        return jnp.concatenate([own_part(j, block, g), halo_kv[32 * j : 32 * j + 32, lanes]], axis=0)

    allowed = []
    for j in range(TILES):
        keys_hot = tile_of(hot, j).astype(BF)
        queries_hot = jnp.concatenate([keys_hot[0:32]] * 4, axis=0)
        allowed.append(lax.dot_general(keys_hot, queries_hot, NT, preferred_element_type=F32) > 0.5)
    scores = [
        lax.dot_general(
            both(j, 1, g), masked_heads(own_part(j, 0, g), 32, 4), NT, preferred_element_type=F32
        )
        for j, g in units
    ]
    probs = [
        softmax_keys(s * scale + bias_ref[half, g], allowed[j]).astype(BF)
        for s, (j, g) in zip(scores, units)
    ]
    outs = [
        lax.dot_general(p, both(j, 2, g), TN, preferred_element_type=F32)
        for p, (j, g) in zip(probs, units)
    ]
    picked = [pick_heads(o, 32, 4).astype(BF) for o in outs]
    return jnp.concatenate(
        [jnp.concatenate(picked[4 * j : 4 * j + 4], axis=1) for j in range(TILES)], axis=0
    )


def half_finish(half, attended, tok_ref, out_ref):
    y = jnp.dot(attended, out_ref[...], preferred_element_type=F32)
    rows = []
    for r in range(4):
        tiles = [y[32 * j + 8 * r : 32 * j + 8 * r + 8] for j in range(TILES)]
        add = jnp.concatenate(tiles, axis=0)[4 : 4 + COLS]
        rows.append((tok_ref[4 * half + r].astype(F32) + add).astype(BF))
    return rows


def pair_kernel(
    halo_ref, frame_ref, inside_ref, side_ref, qkv_ref, bias_ref, tok_ref, out_ref, rows_out, normed
):
    half = 1 - lat_parity()
    attended = half_attend(
        half, halo_ref, frame_ref, inside_ref, side_ref, qkv_ref, bias_ref, False, normed
    )
    for r, row in enumerate(half_finish(half, attended, tok_ref, out_ref)):
        rows_out[r] = row


def cross_kernel(
    halo_ref, frame_ref, inside_ref, side_ref, qkv_ref, bias_ref, tok_ref, out_ref, rows_ref,
    merge_ref, two_ref,
    one_out, merged_out, query_out, kv_out,
    normed, level, parts,
):
    lat = lax.axis_index("lat")
    half = lat_parity()
    outside = (lat == 0) | (lat == lax.axis_size("lat") - 1)
    attended = half_attend(
        half, halo_ref, frame_ref, inside_ref, side_ref, qkv_ref, bias_ref, outside, normed
    )

    def put(row, value):
        one_out[row] = value
        for n in range(4):
            level[n, row] = value[:, n * 128 : n * 128 + 128].astype(F32)

    for r in range(4):
        put(4 * (1 - half) + r, rows_ref[r])
    for r, row in enumerate(half_finish(half, attended, tok_ref, out_ref)):
        put(4 * half + r, row)

    for i in range(4):
        quartet = [
            jnp.concatenate(
                [level[n, 2 * i + dr, pl.ds(dc, COLS // 2, 2), :] for n in range(4)], axis=1
            )
            for dc in range(2)
            for dr in range(2)
        ]
        total = sum(jnp.sum(x, axis=-1, keepdims=True) for x in quartet)
        quartet = [x - total * (1.0 / (4 * D1)) for x in quartet]
        total = sum(jnp.sum(x * x, axis=-1, keepdims=True) for x in quartet)
        factor = lax.rsqrt(total * (1.0 / (4 * D1)) + EPSILON)
        for n in range(4):
            parts[n, :, i] = (quartet[n] * factor).reshape(3, 8, D1)
    merged = jnp.zeros((96, D2), F32)
    for n in range(4):
        merged += jnp.dot(
            parts[n].reshape(96, D1).astype(BF),
            merge_ref[n * D1 : (n + 1) * D1, :],
            preferred_element_type=F32,
        )
    merged = merged.astype(BF)
    merged_out[...] = merged
    x = layer_norm(merged.astype(F32)).astype(BF)
    kv_out[...] = jnp.dot(x, two_ref[:, 512:], preferred_element_type=F32).astype(BF)
    query_out[...] = jnp.dot(x, two_ref[:, :512], preferred_element_type=F32).astype(BF)


def level_two_kernel(
    query_ref, kv_ref, other_ref, merged_ref, bias_ref, out_ref, two_out, keys, result
):
    parity = lat_parity()
    mine = pl.multiple_of(parity * 32, 32)
    theirs = pl.multiple_of(32 - parity * 32, 32)
    scale = LOG2E / math.sqrt(64)
    for w in range(3):
        keys[w, pl.ds(mine, 32), :] = kv_ref[w * 32 : w * 32 + 32, :]
        keys[w, pl.ds(theirs, 32), :] = other_ref[w * 32 : w * 32 + 32, :]
    units = [(w, g) for w in range(3) for g in range(2)]
    scores = [
        lax.dot_general(
            keys[w, :, g * 256 : g * 256 + 256],
            masked_heads(query_ref[w * 32 : w * 32 + 32, g * 256 : g * 256 + 256], 64, 4),
            NT,
            preferred_element_type=F32,
        )
        for w, g in units
    ]
    probs = [
        softmax_keys(s * scale + bias_ref[g], None).astype(BF) for s, (w, g) in zip(scores, units)
    ]
    outs = [
        lax.dot_general(
            p, keys[w, :, 512 + g * 256 : 768 + g * 256], TN, preferred_element_type=F32
        )
        for p, (w, g) in zip(probs, units)
    ]
    picked = [pick_heads(o, 64, 4).astype(BF) for o in outs]
    attended = jnp.concatenate(
        [jnp.concatenate(picked[2 * w : 2 * w + 2], axis=1) for w in range(3)], axis=0
    )
    add = jnp.dot(attended, out_ref[...], preferred_element_type=F32)
    result[...] = (merged_ref[...].astype(F32) + add).reshape(3, 4, 8, D2)
    for i in range(4):
        two_out[i] = result[:, i].reshape(24, D2).astype(BF)


def call(kernel, outs, args, hbm=0, scratch=(), mib=16):
    shapes = [jax.ShapeDtypeStruct(s, d) for s, d in outs]
    place = [pl.BlockSpec(memory_space=pltpu.HBM)] * hbm
    place += [pl.BlockSpec(memory_space=pltpu.VMEM)] * (len(args) - hbm)
    args = [
        pltpu.with_memory_space_constraint(x, pltpu.HBM) if n < hbm else x
        for n, x in enumerate(args)
    ]
    return pl.pallas_call(
        kernel,
        out_shape=shapes,
        in_specs=place,
        out_specs=[pl.BlockSpec(memory_space=pltpu.VMEM)] * len(outs),
        scratch_shapes=list(scratch),
        compiler_params=pltpu.CompilerParams(vmem_limit_bytes=mib * MIB),
        cost_estimate=pl.CostEstimate(flops=1000, bytes_accessed=1000, transcendentals=0),
        name=kernel.__name__,
    )(*args)


def on_device(
    tokens, region_ids, bias_one, qkv_one, out_one, merge_proj, bias_two, qkv_two, out_two
):
    lats, lons = lax.axis_size("lat"), lax.axis_size("lon")
    lat_inner = [(i, i ^ 1) for i in range(lats)]
    lat_outer = [(i, (i + (1 if i % 2 else -1)) % lats) for i in range(lats)]
    lon_inner = [(i, i ^ 1) for i in range(lons)]
    lon_outer = [(i, (i + (1 if i % 2 else -1)) % lons) for i in range(lons)]

    inner, outer, tokens, region_ids = call(
        edge_kernel,
        [((48, D1), BF)] * 2 + [((ROWS, COLS, D1), BF), ((ROWS, COLS), jnp.int32)],
        [tokens, region_ids],
        hbm=2,
        scratch=[pltpu.SemaphoreType.DMA((4,))],
        mib=4,
    )
    inner = lax.ppermute(inner, "lon", lon_inner)
    outer = lax.ppermute(outer, "lon", lon_outer)
    inside, table_one, table_two, qkv_one, out_one, qkv_two = call(
        own_kernel,
        [
            ((2, INSIDE, 32, 3 * D1), BF), ((2, 4, 64, 128), F32), ((2, 64, 128), F32),
            (qkv_one.shape, BF), (out_one.shape, BF), (qkv_two.shape, BF),
        ],
        [qkv_one, bias_one, bias_two, out_one, qkv_two, tokens],
        hbm=5,
        scratch=[
            pltpu.VMEM((2, INSIDE, 2, 16, D1), BF),
            pltpu.VMEM(bias_one.shape, F32),
            pltpu.VMEM(bias_two.shape, F32),
            pltpu.SemaphoreType.DMA((5,)),
        ],
    )
    cross, pair, frame = call(
        band_kernel,
        [((240, D1), BF), ((240, D1), BF), ((ROWS, 128), F32)],
        [tokens, region_ids, inner, outer, table_two],
        mib=8,
    )
    cross = lax.ppermute(cross, "lat", lat_outer)
    pair = lax.ppermute(pair, "lat", lat_inner)
    side, merge_proj, out_two = call(
        side_kernel,
        [((2, 2, 32, 3 * D1), BF), (merge_proj.shape, BF), (out_two.shape, BF)],
        [merge_proj, out_two, tokens, inner, outer, qkv_one, frame],
        hbm=2,
        scratch=[pltpu.SemaphoreType.DMA((2,))],
        mib=8,
    )
    normed = pltpu.VMEM((TILES, 2, 16, D1), BF)
    (pair_rows,) = call(
        pair_kernel,
        [((4, COLS, D1), BF)],
        [pair, frame, inside, side, qkv_one, table_one, tokens, out_one],
        scratch=[normed],
    )
    level_one, merged, query, kv = call(
        cross_kernel,
        [((ROWS, COLS, D1), BF), ((96, D2), BF), ((96, 512), BF), ((96, 1024), BF)],
        [
            cross, frame, inside, side, qkv_one, table_one, tokens, out_one, pair_rows,
            merge_proj, qkv_two,
        ],
        scratch=[
            normed,
            pltpu.VMEM((4, ROWS, COLS, 128), F32),
            pltpu.VMEM((4, 3, 4, 8, D1), F32),
        ],
    )
    other = lax.ppermute(kv, "lat", lat_inner)
    (level_two,) = call(
        level_two_kernel,
        [((4, 24, D2), BF)],
        [query, kv, other, merged, table_two, out_two],
        scratch=[pltpu.VMEM((3, 64, 1024), BF), pltpu.VMEM((3, 4, 8, D2), F32)],
    )
    return (level_one, level_two)


def solution(mesh):
    placed = (P("lat", "lon", None), P("lat", "lon"), P(), P(), P(), P(), P(), P(), P())
    return jax.shard_map(
        on_device,
        mesh=mesh,
        in_specs=placed,
        out_specs=(P("lat", "lon", None), P("lat", "lon", None)),
        check_vma=False,
    )
```

```python
import math

import jax
import jax.numpy as jnp
from jax import lax
from jax.experimental import pallas as pl
from jax.experimental.pallas import tpu as pltpu
from jax.sharding import PartitionSpec as P

EPSILON = 1e-05
LOG2E = math.log2(math.e)
BF = jnp.bfloat16
F32 = jnp.float32
ROWS = 8
COLS = 48
TILES = 7
INSIDE = 5
FRAME = 56
D1 = 512
D2 = 1024
MIB = 1024 * 1024

NT = (((1,), (1,)), ((), ()))
TN = (((0,), (0,)), ((), ()))


def layer_norm(x):
    width = x.shape[-1]
    mean = jnp.sum(x, axis=-1, keepdims=True) * (1.0 / width)
    c = x - mean
    var = jnp.sum(c * c, axis=-1, keepdims=True) * (1.0 / width)
    return c * lax.rsqrt(var + EPSILON)


def lanes_to(x, width):
    return jnp.concatenate([x, jnp.zeros((x.shape[0], width - x.shape[1]), x.dtype)], axis=1)


def lat_parity():
    return lax.rem(lax.axis_index("lat"), 2)


def lon_parity():
    return lax.rem(lax.axis_index("lon"), 2)


def start_all(pairs, sems):
    copies = [pltpu.make_async_copy(src, dst, sems.at[n]) for n, (src, dst) in enumerate(pairs)]
    for copy in copies:
        copy.start()
    return copies


def load_kernel(tok_hbm, ids_hbm, cross_ref, tok_ref, ids_ref, sems):
    for copy in start_all([(ids_hbm, ids_ref), (tok_hbm, tok_ref)], sems):
        copy.wait()
    for r in range(4):
        cross_ref[r * COLS : (r + 1) * COLS] = tok_ref[4 * lat_parity() + r]
    ids = lanes_to(ids_ref[...].astype(F32), D1)
    cross_ref[4 * COLS :] = jnp.where(lat_parity() == 0, ids, pltpu.roll(ids, 4, 0)).astype(BF)


def next_row(r):
    return 4 * lat_parity() + r


def edge_kernel(
    tok_ref, ids_ref, pair_ref, pair_ids_ref, cross_ref, after_ref, inner_ref, outer_ref, all_ids_ref
):
    first = [tok_ref[r, 0:16].astype(F32)[0:4] for r in range(ROWS)]
    first += [pair_ref[next_row(r), 0:16].astype(F32)[0:4] for r in range(4)]
    first += [cross_ref[COLS * r : COLS * r + 16].astype(F32)[0:4] for r in range(4)]
    last = [tok_ref[r, 32:48].astype(F32)[12:16] for r in range(ROWS)]
    last += [pair_ref[next_row(r), 32:48].astype(F32)[12:16] for r in range(4)]
    last += [cross_ref[COLS * r + 32 : COLS * r + 48].astype(F32)[12:16] for r in range(4)]
    own = lanes_to(ids_ref[...].astype(F32), 128)
    pair = lanes_to(pair_ids_ref[...].astype(F32), 128)
    pair = jnp.where(lat_parity() == 0, pair, pltpu.roll(pair, 4, 0))
    cross = cross_ref[4 * COLS :, 0:128].astype(F32)
    halo = jnp.concatenate([pair[0:4], cross[0:4]], axis=0)
    all_ids_ref[...] = jnp.concatenate([own, halo], axis=0)
    ids = jnp.concatenate([own, halo], axis=1)
    first = jnp.concatenate(first + [lanes_to(ids, D1)], axis=0).astype(BF)
    ids = pltpu.roll(ids, 256 - (COLS - 4), 1)
    last = jnp.concatenate(last + [lanes_to(ids, D1)], axis=0).astype(BF)
    even = lon_parity() == 0
    inner_ref[...] = jnp.where(even, last, first)
    outer_ref[...] = jnp.where(even, first, last)


def sides(inner_ref, outer_ref):
    inner, outer = inner_ref[...].astype(F32), outer_ref[...].astype(F32)
    even = lon_parity() == 0
    return jnp.where(even, outer, inner), jnp.where(even, inner, outer)


def own_kernel(qkv_ref, one_ref, two_ref, tok_ref, inside_out, one_out, two_out, normed):
    for r in range(0, ROWS, 2):
        pair = []
        for k in range(2):
            x = layer_norm(tok_ref[r + k].astype(F32))
            pair.append(x[4 : COLS - 4].reshape(INSIDE, 8, D1))
        normed[r // 4, :, (r % 4) // 2] = jnp.concatenate(pair, axis=1).astype(BF)
    for half in range(2):
        low = 32 * (1 - half)
        for g in range(4):
            turned = one_ref[4 * g : 4 * g + 4, low : low + 32, :].reshape(128, 64).T * LOG2E
            one_out[half, g, 0:32] = turned[low : low + 32]
            one_out[half, g, 32:64] = turned[32 - low : 64 - low]
    low = pl.multiple_of(lat_parity() * 32, 32)
    for g in range(2):
        turned = two_ref[4 * g : 4 * g + 4, pl.ds(low, 32), :].reshape(128, 64).T * LOG2E
        even = lat_parity() == 0
        two_out[g, 0:32] = jnp.where(even, turned[0:32], turned[32:64])
        two_out[g, 32:64] = jnp.where(even, turned[32:64], turned[0:32])
    x = normed[...].reshape(2 * INSIDE * 32, D1)
    inside_out[...] = (
        jnp.dot(x, qkv_ref[...], preferred_element_type=F32)
        .astype(BF)
        .reshape(2, INSIDE, 32, 3 * D1)
    )


def masked_heads(q, head_dim, count):
    lane = lax.broadcasted_iota(jnp.int32, q.shape, 1) // head_dim
    zero = jnp.zeros_like(q)
    return jnp.concatenate([jnp.where(lane == h, q, zero) for h in range(count)], axis=0)


def pick_heads(o, head_dim, count):
    rows = o.shape[0] // count
    lane = lax.broadcasted_iota(jnp.int32, (rows, o.shape[1]), 1) // head_dim
    out = o[0:rows]
    for h in range(1, count):
        out = jnp.where(lane == h, o[h * rows : (h + 1) * rows], out)
    return out


def softmax_keys(s, allowed):
    if allowed is not None:
        s = jnp.where(allowed, s, -1e30)
    p = jnp.exp2(s - jnp.max(s, axis=0, keepdims=True))
    return p * (1.0 / jnp.sum(p, axis=0, keepdims=True))


def region_masks(ids):
    lat = lax.axis_index("lat")
    outside = (lat == 0) | (lat == lax.axis_size("lat") - 1)
    pair = ids[8:12]
    cross = jnp.where(outside, -1.0, ids[12:16])
    even = lat_parity() == 0
    above, below = jnp.where(even, cross, pair), jnp.where(even, pair, cross)
    rows = [ids[0:4], above, ids[4:8], below, jnp.zeros((112, 128), F32)]
    turned = jnp.concatenate(rows, axis=0).T

    def window(half, j):
        tiles = [
            jnp.broadcast_to(turned[8 * j : 8 * j + 8, r : r + 1], (8, 128))
            for r in range(8 * half, 8 * half + 8)
        ]
        queries = jnp.concatenate(tiles[0:4] * 4, axis=0).T[0:1]
        return jnp.concatenate(tiles, axis=0) == queries

    return window


def attend_one(windows, mask, bias_ref, query, keys, values):
    scale = LOG2E / math.sqrt(32)
    units = [(w, g) for w in range(len(windows)) for g in range(4)]
    allowed = [mask(half, j) for half, j in windows]
    scores = [
        lax.dot_general(
            keys(w, g), masked_heads(query(w, g), 32, 4), NT, preferred_element_type=F32
        )
        for w, g in units
    ]
    probs = [
        softmax_keys(s * scale + bias_ref[windows[w][0], g], allowed[w]).astype(BF)
        for s, (w, g) in zip(scores, units)
    ]
    outs = [
        lax.dot_general(p, values(w, g), TN, preferred_element_type=F32)
        for p, (w, g) in zip(probs, units)
    ]
    picked = [pick_heads(o, 32, 4).astype(BF) for o in outs]
    return [jnp.concatenate(picked[4 * w : 4 * w + 4], axis=1) for w in range(len(windows))]


def lanes_of(block, g):
    return slice(block * D1 + g * 128, block * D1 + g * 128 + 128)


def inner_kernel(
    pair_ref, cross_ref, ids_ref, inside_ref, qkv_ref, bias_ref, out_ref, add_out, normed
):
    even = lat_parity() == 0
    for half in range(2):
        for r in range(0, 4, 2):
            rows = []
            for k in range(r, r + 2):
                pair = pair_ref[next_row(k)].astype(F32)
                cross = cross_ref[COLS * k : COLS * k + COLS].astype(F32)
                x = jnp.where(even, cross, pair) if half == 0 else jnp.where(even, pair, cross)
                rows.append(layer_norm(x)[4 : COLS - 4].reshape(INSIDE, 8, D1))
            normed[half, :, r // 2] = jnp.concatenate(rows, axis=1).astype(BF)
    halo = jnp.dot(
        normed[...].reshape(2 * INSIDE * 32, D1), qkv_ref[:, D1:], preferred_element_type=F32
    ).astype(BF)
    windows = [(half, j) for half in range(2) for j in range(1, TILES - 1)]

    def both(w, block, g):
        half, j = windows[w]
        own = inside_ref[half, j - 1, :, lanes_of(block, g)]
        return jnp.concatenate([own, halo[32 * w : 32 * w + 32, lanes_of(block - 1, g)]], axis=0)

    attended = attend_one(
        windows,
        region_masks(pltpu.roll(ids_ref[...], 4, 1)),
        bias_ref,
        lambda w, g: inside_ref[windows[w][0], windows[w][1] - 1, :, lanes_of(0, g)],
        lambda w, g: both(w, 1, g),
        lambda w, g: both(w, 2, g),
    )
    add_out[...] = jnp.dot(
        jnp.concatenate(attended, axis=0), out_ref[...], preferred_element_type=F32
    )


def final_kernel(
    tok_ref, pair_ref, cross_ref, inner_ref, outer_ref, ids_ref, qkv_ref, bias_ref, out_ref,
    add_ref, merge_ref, two_ref,
    one_out, merged_out, normed_out, kv_out,
    level, parts,
):
    even = lat_parity() == 0
    west, east = sides(inner_ref, outer_ref)
    lane = lax.broadcasted_iota(jnp.int32, (2 * ROWS, 128), 1)
    own = pltpu.roll(ids_ref[...], 4, 1)
    near = jnp.concatenate([west[64:72, 0:128], west[64:72, 128:256]], axis=0)
    far = jnp.concatenate([east[64:72, 0:128], east[64:72, 128:256]], axis=0)
    far = pltpu.roll(far, COLS + 4, 1)
    ids = jnp.where(lane < 4, near, jnp.where(lane < COLS + 4, own, far))

    first = [tok_ref[r, 0:16].astype(F32)[0:4] for r in range(ROWS)]
    first += [pair_ref[next_row(r), 0:16].astype(F32)[0:4] for r in range(4)]
    first += [cross_ref[COLS * r : COLS * r + 16].astype(F32)[0:4] for r in range(4)]
    last = [tok_ref[r, 32:48].astype(F32)[12:16] for r in range(ROWS)]
    last += [pair_ref[next_row(r), 32:48].astype(F32)[12:16] for r in range(4)]
    last += [cross_ref[COLS * r + 32 : COLS * r + 48].astype(F32)[12:16] for r in range(4)]
    tiles = []
    for side in range(2):
        rows = []
        for r in range(2 * ROWS):
            if side == 0:
                rows += [west[4 * r : 4 * r + 4], first[r]]
            else:
                rows += [last[r], east[4 * r : 4 * r + 4]]
        tiles.append(layer_norm(jnp.concatenate(rows, axis=0)))
    windows = [(half, j) for half in range(2) for j in (0, TILES - 1)]
    ordered = []
    for half, j in windows:
        x = tiles[j // (TILES - 1)]
        a, b = (x[96:128], x[64:96]) if half == 0 else (x[64:96], x[96:128])
        ordered += [x[32 * half : 32 * half + 32], jnp.where(even, a, b)]
    qkv = jnp.dot(
        jnp.concatenate(ordered, axis=0).astype(BF), qkv_ref[...], preferred_element_type=F32
    ).astype(BF)
    attended = attend_one(
        windows,
        region_masks(ids),
        bias_ref,
        lambda w, g: qkv[64 * w : 64 * w + 32, lanes_of(0, g)],
        lambda w, g: qkv[64 * w : 64 * w + 64, lanes_of(1, g)],
        lambda w, g: qkv[64 * w : 64 * w + 64, lanes_of(2, g)],
    )
    edge = jnp.dot(jnp.concatenate(attended, axis=0), out_ref[...], preferred_element_type=F32)
    for row in range(ROWS):
        half, r = row // 4, row % 4
        adds = [edge[64 * half + 8 * r : 64 * half + 8 * r + 8]]
        for j in range(INSIDE):
            at = 32 * (INSIDE * half + j) + 8 * r
            adds.append(add_ref[at : at + 8])
        adds.append(edge[64 * half + 32 + 8 * r : 64 * half + 40 + 8 * r])
        add = jnp.concatenate(adds, axis=0)[4 : 4 + COLS]
        value = (tok_ref[row].astype(F32) + add).astype(BF)
        one_out[row] = value
        for n in range(4):
            level[n, row] = value[:, n * 128 : n * 128 + 128].astype(F32)

    for i in range(4):
        quartet = [
            jnp.concatenate(
                [level[n, 2 * i + dr, pl.ds(dc, COLS // 2, 2), :] for n in range(4)], axis=1
            )
            for dc in range(2)
            for dr in range(2)
        ]
        total = sum(jnp.sum(x, axis=-1, keepdims=True) for x in quartet)
        quartet = [x - total * (1.0 / (4 * D1)) for x in quartet]
        total = sum(jnp.sum(x * x, axis=-1, keepdims=True) for x in quartet)
        factor = lax.rsqrt(total * (1.0 / (4 * D1)) + EPSILON)
        for n in range(4):
            parts[n, :, i] = (quartet[n] * factor).reshape(3, 8, D1)
    merged = jnp.zeros((96, D2), F32)
    for n in range(4):
        merged += jnp.dot(
            parts[n].reshape(96, D1).astype(BF),
            merge_ref[n * D1 : (n + 1) * D1, :],
            preferred_element_type=F32,
        )
    merged = merged.astype(BF)
    merged_out[...] = merged
    x = layer_norm(merged.astype(F32)).astype(BF)
    normed_out[...] = x
    kv_out[...] = jnp.dot(x, two_ref[:, 512:], preferred_element_type=F32).astype(BF)


TWO_UNITS = [(w, g) for w in range(3) for g in range(2)]


def scores_two(keys_ref, queries, bias):
    scale = LOG2E / math.sqrt(64)
    return [
        lax.dot_general(
            keys_ref[w * 32 : w * 32 + 32, g * 256 : g * 256 + 256],
            masked_heads(queries[w * 32 : w * 32 + 32, g * 256 : g * 256 + 256], 64, 4),
            NT,
            preferred_element_type=F32,
        )
        * scale
        + bias[g]
        for w, g in TWO_UNITS
    ]


def query_kernel(normed_ref, kv_ref, bias_ref, two_ref, query_out, score_out):
    q = jnp.dot(normed_ref[...], two_ref[:, :512], preferred_element_type=F32).astype(BF)
    query_out[...] = q
    for n, s in enumerate(scores_two(kv_ref, q, [bias_ref[g, 0:32] for g in range(2)])):
        score_out[n] = s


def level_two_kernel(
    query_ref, score_ref, kv_ref, other_ref, merged_ref, bias_ref, out_ref, two_out
):
    far = scores_two(other_ref, query_ref[...], [bias_ref[g, 32:64] for g in range(2)])
    probs = [
        softmax_keys(jnp.concatenate([score_ref[n], s], axis=0), None).astype(BF)
        for n, s in enumerate(far)
    ]
    outs = []
    for p, (w, g) in zip(probs, TWO_UNITS):
        block = (slice(w * 32, w * 32 + 32), slice(512 + g * 256, 768 + g * 256))
        values = jnp.concatenate([kv_ref[block], other_ref[block]], axis=0)
        outs.append(lax.dot_general(p, values, TN, preferred_element_type=F32))
    picked = [pick_heads(o, 64, 4).astype(BF) for o in outs]
    attended = jnp.concatenate(
        [jnp.concatenate(picked[2 * w : 2 * w + 2], axis=1) for w in range(3)], axis=0
    )
    y = merged_ref[...].astype(F32) + jnp.dot(
        attended, out_ref[...], preferred_element_type=F32
    )
    for i in range(4):
        tiles = [y[32 * w + 8 * i : 32 * w + 8 * i + 8] for w in range(3)]
        two_out[i] = jnp.concatenate(tiles, axis=0).astype(BF)


def call(kernel, outs, args, hbm=0, scratch=(), mib=16, us=1.0):
    shapes = [jax.ShapeDtypeStruct(s, d) for s, d in outs]
    place = [pl.BlockSpec(memory_space=pltpu.HBM)] * hbm
    place += [pl.BlockSpec(memory_space=pltpu.VMEM)] * (len(args) - hbm)
    args = [
        pltpu.with_memory_space_constraint(x, pltpu.HBM) if n < hbm else x
        for n, x in enumerate(args)
    ]
    return pl.pallas_call(
        kernel,
        out_shape=shapes,
        in_specs=place,
        out_specs=[pl.BlockSpec(memory_space=pltpu.VMEM)] * len(outs),
        scratch_shapes=list(scratch),
        compiler_params=pltpu.CompilerParams(vmem_limit_bytes=mib * MIB),
        cost_estimate=pl.CostEstimate(
            flops=int(us * 10**9), bytes_accessed=10**6, transcendentals=0
        ),
        name=kernel.__name__,
    )(*args)


def on_device(
    tokens, region_ids, bias_one, qkv_one, out_one, merge_proj, bias_two, qkv_two, out_two
):
    lats, lons = lax.axis_size("lat"), lax.axis_size("lon")
    lat_inner = [(i, i ^ 1) for i in range(lats)]
    lat_outer = [(i, (i + (1 if i % 2 else -1)) % lats) for i in range(lats)]
    lon_inner = [(i, i ^ 1) for i in range(lons)]
    lon_outer = [(i, (i + (1 if i % 2 else -1)) % lons) for i in range(lons)]

    pair = lax.ppermute(tokens, "lat", lat_inner)
    pair_ids = lax.ppermute(region_ids, "lat", lat_inner)
    cross, tokens, region_ids = call(
        load_kernel,
        [((200, D1), BF), ((ROWS, COLS, D1), BF), ((ROWS, COLS), jnp.int32)],
        [tokens, region_ids],
        hbm=2,
        scratch=[pltpu.SemaphoreType.DMA((2,))],
        mib=4,
        us=4.0,
    )
    cross = lax.ppermute(cross, "lat", lat_outer)
    inside, table_one, table_two = call(
        own_kernel,
        [((2, INSIDE, 32, 3 * D1), BF), ((2, 4, 64, 128), F32), ((2, 64, 128), F32)],
        [qkv_one, bias_one, bias_two, tokens],
        scratch=[pltpu.VMEM((2, INSIDE, 2, 16, D1), BF)],
        us=1.5,
    )
    inner, outer, ids = call(
        edge_kernel,
        [((72, D1), BF), ((72, D1), BF), ((2 * ROWS, 128), F32)],
        [tokens, region_ids, pair, pair_ids, cross, table_two],
        mib=4,
    )
    inner = lax.ppermute(inner, "lon", lon_inner)
    outer = lax.ppermute(outer, "lon", lon_outer)
    (added,) = call(
        inner_kernel,
        [((2 * INSIDE * 32, D1), F32)],
        [pair, cross, ids, inside, qkv_one, table_one, out_one],
        scratch=[pltpu.VMEM((2, INSIDE, 2, 16, D1), BF)],
        us=0.3,
    )
    level_one, merged, normed, kv = call(
        final_kernel,
        [((ROWS, COLS, D1), BF), ((96, D2), BF), ((96, D2), BF), ((96, 1024), BF)],
        [
            tokens, pair, cross, inner, outer, ids, qkv_one, table_one, out_one, added,
            merge_proj, qkv_two,
        ],
        scratch=[pltpu.VMEM((4, ROWS, COLS, 128), F32), pltpu.VMEM((4, 3, 4, 8, D1), F32)],
    )
    other_kv = lax.ppermute(kv, "lat", lat_inner)
    query, scores = call(
        query_kernel,
        [((96, 512), BF), ((6, 32, 128), F32)],
        [normed, kv, table_two, qkv_two],
    )
    (level_two,) = call(
        level_two_kernel,
        [((4, 24, D2), BF)],
        [query, scores, kv, other_kv, merged, table_two, out_two],
    )
    return (level_one, level_two)


def solution(mesh):
    placed = (P("lat", "lon", None), P("lat", "lon"), P(), P(), P(), P(), P(), P(), P())
    return jax.shard_map(
        on_device,
        mesh=mesh,
        in_specs=placed,
        out_specs=(P("lat", "lon", None), P("lat", "lon", None)),
        check_vma=False,
    )
```

```python
import math

import jax
import jax.numpy as jnp
from jax import lax
from jax.experimental import pallas as pl
from jax.experimental.pallas import tpu as pltpu
from jax.sharding import PartitionSpec as P

EPSILON = 1e-05
LOG2E = math.log2(math.e)
BF = jnp.bfloat16
F32 = jnp.float32
ROWS = 8
COLS = 48
TILES = 7
INSIDE = 5
FRAME = 56
D1 = 512
D2 = 1024
MIB = 1024 * 1024

NT = (((1,), (1,)), ((), ()))
TN = (((0,), (0,)), ((), ()))


def layer_norm(x):
    width = x.shape[-1]
    mean = jnp.sum(x, axis=-1, keepdims=True) * (1.0 / width)
    c = x - mean
    var = jnp.sum(c * c, axis=-1, keepdims=True) * (1.0 / width)
    return c * lax.rsqrt(var + EPSILON)


def row_stats(blocks):
    width = sum(x.shape[-1] for x in blocks)
    mean = sum(jnp.sum(x, axis=-1, keepdims=True) for x in blocks) * (1.0 / width)
    centered = [x - mean for x in blocks]
    var = sum(jnp.sum(c * c, axis=-1, keepdims=True) for c in centered) * (1.0 / width)
    return mean, lax.rsqrt(var + EPSILON)


def lanes_to(x, width):
    return jnp.concatenate([x, jnp.zeros((x.shape[0], width - x.shape[1]), x.dtype)], axis=1)


def lat_parity():
    return lax.rem(lax.axis_index("lat"), 2)


def lon_parity():
    return lax.rem(lax.axis_index("lon"), 2)


def start_all(pairs, sems):
    copies = [pltpu.make_async_copy(src, dst, sems.at[n]) for n, (src, dst) in enumerate(pairs)]
    for copy in copies:
        copy.start()
    return copies


def load_kernel(tok_hbm, ids_hbm, cross_ref, tok_ref, ids_ref, sems):
    copies = start_all([(ids_hbm, ids_ref), (tok_hbm, tok_ref)], sems)
    copies[0].wait()
    ids = lanes_to(ids_ref[...].astype(F32), D1)
    cross_ref[4 * COLS :] = jnp.where(lat_parity() == 0, ids, pltpu.roll(ids, 4, 0)).astype(BF)
    copies[1].wait()
    for r in range(4):
        cross_ref[r * COLS : (r + 1) * COLS] = tok_ref[4 * lat_parity() + r]


def next_row(r):
    return 4 * lat_parity() + r


def edge_kernel(
    tok_ref, ids_ref, pair_ref, pair_ids_ref, cross_ref, after_ref, inner_ref, outer_ref, all_ids_ref
):
    first = [tok_ref[r, 0:16].astype(F32)[0:4] for r in range(ROWS)]
    first += [pair_ref[next_row(r), 0:16].astype(F32)[0:4] for r in range(4)]
    first += [cross_ref[COLS * r : COLS * r + 16].astype(F32)[0:4] for r in range(4)]
    last = [tok_ref[r, 32:48].astype(F32)[12:16] for r in range(ROWS)]
    last += [pair_ref[next_row(r), 32:48].astype(F32)[12:16] for r in range(4)]
    last += [cross_ref[COLS * r + 32 : COLS * r + 48].astype(F32)[12:16] for r in range(4)]
    own = lanes_to(ids_ref[...].astype(F32), 128)
    pair = lanes_to(pair_ids_ref[...].astype(F32), 128)
    pair = jnp.where(lat_parity() == 0, pair, pltpu.roll(pair, 4, 0))
    cross = cross_ref[4 * COLS :, 0:128].astype(F32)
    halo = jnp.concatenate([pair[0:4], cross[0:4]], axis=0)
    all_ids_ref[...] = jnp.concatenate([own, halo], axis=0)
    ids = jnp.concatenate([own, halo], axis=1)
    first = jnp.concatenate(first + [lanes_to(ids, D1)], axis=0).astype(BF)
    ids = pltpu.roll(ids, 256 - (COLS - 4), 1)
    last = jnp.concatenate(last + [lanes_to(ids, D1)], axis=0).astype(BF)
    even = lon_parity() == 0
    inner_ref[...] = jnp.where(even, last, first)
    outer_ref[...] = jnp.where(even, first, last)


def sides(inner_ref, outer_ref):
    inner, outer = inner_ref[...].astype(F32), outer_ref[...].astype(F32)
    even = lon_parity() == 0
    return jnp.where(even, outer, inner), jnp.where(even, inner, outer)


def side_pieces(x, row):
    order = [row + r for r in range(4)] + [4 - row + r for r in range(4)]
    west = [x[8 * r + c : 8 * r + c + 4] for c in (4, 0) for r in order]
    east = [x[8 * r + c : 8 * r + c + 4] for c in (0, 4) for r in order]
    return west, east


def own_kernel(
    qkv_ref, one_ref, two_ref, tok_ref, inside_out, edge_out, one_out, side_out, two_out, normed
):
    first, last = [], []
    for r in range(0, ROWS, 2):
        pair = []
        for k in range(2):
            x = layer_norm(tok_ref[r + k].astype(F32))
            pair.append(x[4 : COLS - 4].reshape(INSIDE, 8, D1))
            first.append(x[0:4])
            last.append(x[COLS - 4 :])
        normed[r // 4, :, (r % 4) // 2] = jnp.concatenate(pair, axis=1).astype(BF)
    edge = jnp.concatenate(first[0:4] + last[0:4] + first[4:8] + last[4:8], axis=0).astype(BF)
    for half in range(2):
        low = 32 * (1 - half)
        for g in range(4):
            turned = one_ref[4 * g : 4 * g + 4, low : low + 32, :].reshape(128, 64).T * LOG2E
            one_out[half, g, 0:32] = turned[low : low + 32]
            one_out[half, g, 32:64] = turned[32 - low : 64 - low]
    for half in range(2):
        row = 4 * (1 - half)
        for g in range(2):
            heads = [side_pieces(one_ref[8 * g + h], row) for h in range(8)]
            for side in range(2):
                part = jnp.concatenate([x for h in heads for x in h[side][0:4]], axis=0)
                pieces = side_pieces(part.T * LOG2E, row)[side]
                side_out[half, side, g] = jnp.concatenate(pieces, axis=0)
    low = pl.multiple_of(lat_parity() * 32, 32)
    for g in range(2):
        turned = two_ref[4 * g : 4 * g + 4, pl.ds(low, 32), :].reshape(128, 64).T * LOG2E
        even = lat_parity() == 0
        two_out[g, 0:32] = jnp.where(even, turned[0:32], turned[32:64])
        two_out[g, 32:64] = jnp.where(even, turned[32:64], turned[0:32])
    x = jnp.concatenate([normed[...].reshape(2 * INSIDE * 32, D1), edge], axis=0)
    qkv = jnp.dot(x, qkv_ref[...], preferred_element_type=F32).astype(BF)
    inside_out[...] = qkv[0 : 2 * INSIDE * 32].reshape(2, INSIDE, 32, 3 * D1)
    edge_out[...] = qkv[2 * INSIDE * 32 :]


def masked_heads(q, head_dim, count):
    lane = lax.broadcasted_iota(jnp.int32, q.shape, 1) // head_dim
    zero = jnp.zeros_like(q)
    return jnp.concatenate([jnp.where(lane == h, q, zero) for h in range(count)], axis=0)


def pick_heads(o, head_dim, count):
    rows = o.shape[0] // count
    lane = lax.broadcasted_iota(jnp.int32, (rows, o.shape[1]), 1) // head_dim
    out = o[0:rows]
    for h in range(1, count):
        out = jnp.where(lane == h, o[h * rows : (h + 1) * rows], out)
    return out


def softmax_keys(s, allowed):
    if allowed is not None:
        s = jnp.where(allowed, s, -1e30)
    p = jnp.exp2(s - jnp.max(s, axis=0, keepdims=True))
    return p * (1.0 / jnp.sum(p, axis=0, keepdims=True))


def region_masks(own, halo):
    turned = jnp.concatenate([own, halo, jnp.zeros((120, 128), F32)], axis=0).T

    def window(j):
        tiles = [
            jnp.broadcast_to(turned[8 * j : 8 * j + 8, r : r + 1], (8, 128)) for r in range(8)
        ]
        queries = jnp.concatenate(tiles[0:4] * 4, axis=0).T[0:1]
        return jnp.concatenate(tiles, axis=0) == queries

    return window


def in_range(cross_ids):
    lat = lax.axis_index("lat")
    outside = (lat == 0) | (lat == lax.axis_size("lat") - 1)
    return jnp.where(outside, -1.0, cross_ids)


def attend_one(halves, allowed, bias_ref, query, keys, values):
    scale = LOG2E / math.sqrt(32)
    units = [(w, g) for w in range(len(halves)) for g in range(4)]
    scores = [
        lax.dot_general(
            keys(w, g), masked_heads(query(w, g), 32, 4), NT, preferred_element_type=F32
        )
        for w, g in units
    ]
    probs = [
        softmax_keys(s * scale + bias_ref[halves[w], g], allowed[w]).astype(BF)
        for s, (w, g) in zip(scores, units)
    ]
    outs = [
        lax.dot_general(p, values(w, g), TN, preferred_element_type=F32)
        for p, (w, g) in zip(probs, units)
    ]
    picked = [pick_heads(o, 32, 4).astype(BF) for o in outs]
    return [jnp.concatenate(picked[4 * w : 4 * w + 4], axis=1) for w in range(len(halves))]


def lanes_of(block, g):
    return slice(block * D1 + g * 128, block * D1 + g * 128 + 128)


def half_inner(half, halo_rows, own_ids, halo_ids, inside_ref, qkv_ref, bias_ref, out_ref, normed):
    rows = [layer_norm(x) for x in halo_rows]
    for r in range(0, 4, 2):
        pair = [rows[k][4 : COLS - 4].reshape(INSIDE, 8, D1) for k in (r, r + 1)]
        normed[:, r // 2] = jnp.concatenate(pair, axis=1).astype(BF)
    edge = jnp.concatenate([x[0:4] for x in rows] + [x[COLS - 4 :] for x in rows], axis=0)
    halo = jnp.dot(
        jnp.concatenate([normed[...].reshape(INSIDE * 32, D1), edge.astype(BF)], axis=0),
        qkv_ref[:, D1:],
        preferred_element_type=F32,
    ).astype(BF)
    mask = region_masks(pltpu.roll(own_ids, 4, 1), pltpu.roll(halo_ids, 4, 1))

    def both(w, block, g):
        own = inside_ref[half, w, :, lanes_of(block, g)]
        return jnp.concatenate([own, halo[32 * w : 32 * w + 32, lanes_of(block - 1, g)]], axis=0)

    attended = attend_one(
        [half] * INSIDE,
        [mask(j) for j in range(1, TILES - 1)],
        bias_ref,
        lambda w, g: inside_ref[half, w, :, lanes_of(0, g)],
        lambda w, g: both(w, 1, g),
        lambda w, g: both(w, 2, g),
    )
    add = jnp.dot(jnp.concatenate(attended, axis=0), out_ref[...], preferred_element_type=F32)
    return add, halo[INSIDE * 32 :]


def pair_kernel(
    pair_ref, pair_ids_ref, ids_ref, inside_ref, qkv_ref, bias_ref, out_ref, add_out, edge_out,
    normed,
):
    even = lat_parity() == 0
    own = lanes_to(ids_ref[...].astype(F32), 128)
    pair = lanes_to(pair_ids_ref[...].astype(F32), 128)
    own = jnp.where(even, pltpu.roll(own, 4, 0), own)
    pair = jnp.where(even, pair, pltpu.roll(pair, 4, 0))
    rows = [pair_ref[next_row(r)].astype(F32) for r in range(4)]
    add_out[...], edge_out[...] = half_inner(
        1 - lat_parity(), rows, own[0:4], pair[0:4], inside_ref, qkv_ref, bias_ref, out_ref, normed
    )


def cross_kernel(
    cross_ref, ids_ref, inside_ref, qkv_ref, bias_ref, out_ref, add_out, edge_out, normed
):
    ids = ids_ref[...]
    own = jnp.where(lat_parity() == 0, ids[0:4], ids[4:8])
    rows = [cross_ref[COLS * r : COLS * r + COLS].astype(F32) for r in range(4)]
    add_out[...], edge_out[...] = half_inner(
        lat_parity(), rows, own, in_range(ids[12:16]), inside_ref, qkv_ref, bias_ref, out_ref, normed
    )


def final_kernel(
    tok_ref, inner_ref, outer_ref, ids_ref, qkv_ref, bias_ref, out_ref, own_edge_ref,
    pair_edge_ref, cross_edge_ref, pair_add_ref, cross_add_ref, merge_ref, two_ref,
    merge_sum_ref, two_sum_ref,
    one_out, merged_out, kv_out,
    level, parts, done, sem,
):
    even = lat_parity() == 0
    west, east = sides(inner_ref, outer_ref)
    x = layer_norm(jnp.concatenate([west[0:64], east[0:64]], axis=0)).astype(BF)
    new = jnp.dot(x, qkv_ref[:, D1:], preferred_element_type=F32).astype(BF)

    lane = lax.broadcasted_iota(jnp.int32, (2 * ROWS, 128), 1)
    own = pltpu.roll(ids_ref[...], 4, 1)
    near = jnp.concatenate([west[64:72, 0:128], west[64:72, 128:256]], axis=0)
    far = jnp.concatenate([east[64:72, 0:128], east[64:72, 128:256]], axis=0)
    far = pltpu.roll(far, COLS + 4, 1)
    ids = jnp.where(lane < 4, near, jnp.where(lane < COLS + 4, own, far))
    pair_ids, cross_ids = ids[8:12], in_range(ids[12:16])
    above, below = jnp.where(even, cross_ids, pair_ids), jnp.where(even, pair_ids, cross_ids)
    rows = [ids[0:4], above, ids[4:8], below, jnp.zeros((112, 128), F32)]
    turned = jnp.concatenate(rows, axis=0).T

    windows = [(half, side) for half in range(2) for side in range(2)]
    keys, values, queries, allowed = [], [], [], []
    for half, side in windows:
        at = 16 * (2 * half + side)
        a, b = cross_edge_ref, pair_edge_ref
        c, d = new[64 * side + 48 : 64 * side + 64], new[64 * side + 32 : 64 * side + 48]
        if half == 1:
            a, b, c, d = b, a, d, c
        lines = slice(16 * side, 16 * side + 16)
        kv = jnp.concatenate(
            [
                own_edge_ref[at : at + 16, D1:],
                jnp.where(even, a[lines], b[lines]),
                new[64 * side + 16 * half : 64 * side + 16 * half + 16],
                jnp.where(even, c, d),
            ],
            axis=0,
        )
        keys.append(kv[:, 0:D1])
        values.append(kv[:, D1:])
        queries.append(own_edge_ref[at : at + 16, 0:D1])
        starts = (4, 0) if side == 0 else (COLS, COLS + 4)
        pieces = [
            jnp.broadcast_to(turned[c0 : c0 + 4, r : r + 1], (4, 128))
            for c0 in starts
            for r in range(8 * half, 8 * half + 8)
        ]
        own_ids = jnp.concatenate(pieces[0:4] * 8, axis=0).T[0:1]
        allowed.append(jnp.concatenate(pieces, axis=0) == own_ids)
    scale = LOG2E / math.sqrt(32)
    units = [(w, g) for w in range(4) for g in range(2)]
    scores = [
        lax.dot_general(
            keys[w][:, 256 * g : 256 * g + 256],
            masked_heads(queries[w][:, 256 * g : 256 * g + 256], 32, 8),
            NT,
            preferred_element_type=F32,
        )
        for w, g in units
    ]
    probs = [
        softmax_keys(s * scale + bias_ref[windows[w][0], windows[w][1], g], allowed[w]).astype(BF)
        for s, (w, g) in zip(scores, units)
    ]
    outs = [
        lax.dot_general(p, values[w][:, 256 * g : 256 * g + 256], TN, preferred_element_type=F32)
        for p, (w, g) in zip(probs, units)
    ]
    picked = [pick_heads(o, 32, 8).astype(BF) for o in outs]
    attended = [jnp.concatenate(picked[2 * w : 2 * w + 2], axis=1) for w in range(4)]
    edge = jnp.dot(jnp.concatenate(attended, axis=0), out_ref[...], preferred_element_type=F32)
    for row in range(ROWS):
        half, r = row // 4, row % 4
        at = 32 * half + 4 * r
        adds = [edge[at : at + 4]]
        for j in range(INSIDE):
            tile = slice(32 * j + 8 * r, 32 * j + 8 * r + 8)
            upper, lower = cross_add_ref[tile], pair_add_ref[tile]
            if half == 1:
                upper, lower = lower, upper
            adds.append(jnp.where(even, upper, lower))
        adds.append(edge[at + 16 : at + 20])
        value = (tok_ref[row].astype(F32) + jnp.concatenate(adds, axis=0)).astype(BF)
        done[row] = value
        for n in range(4):
            level[n, row] = value[:, n * 128 : n * 128 + 128].astype(F32)
    store = pltpu.make_async_copy(done, one_out, sem)
    store.start()

    means, factors = [], []
    for i in range(4):
        quartet = [
            jnp.concatenate(
                [level[n, 2 * i + dr, pl.ds(dc, COLS // 2, 2), :] for n in range(4)], axis=1
            )
            for dc in range(2)
            for dr in range(2)
        ]
        for n in range(4):
            parts[n, :, i] = quartet[n].reshape(3, 8, D1)
        mean, factor = row_stats(quartet)
        means.append(mean)
        factors.append(factor)
    order = [(i, slice(8 * w, 8 * w + 8)) for w in range(3) for i in range(4)]
    mean = jnp.concatenate([means[i][at] for i, at in order], axis=0)
    factor = jnp.concatenate([factors[i][at] for i, at in order], axis=0)
    total = jnp.zeros((96, D2), F32)
    for n in range(4):
        total += jnp.dot(
            parts[n].reshape(96, D1).astype(BF),
            merge_ref[n * D1 : (n + 1) * D1, :],
            preferred_element_type=F32,
        )
    merged = ((total - mean * merge_sum_ref[0:1]) * factor).astype(BF)
    merged_out[...] = merged
    mean, factor = row_stats([merged.astype(F32)])
    total = jnp.dot(merged, two_ref[:, 512:], preferred_element_type=F32)
    kv_out[...] = ((total - mean * two_sum_ref[0:1, 512:]) * factor).astype(BF)
    store.wait()


def sums_kernel(merge_ref, two_ref, after_ref, merge_out, two_out):
    ones = jnp.ones((16, 4 * D1), BF)
    merge_out[...] = jnp.dot(ones, merge_ref[...], preferred_element_type=F32)[0:8]
    two_out[...] = jnp.dot(ones[:, 0:D2], two_ref[...], preferred_element_type=F32)[0:8]


TWO_UNITS = [(w, g) for w in range(3) for g in range(2)]


def scores_two(keys_ref, queries, bias):
    scale = LOG2E / math.sqrt(64)
    return [
        lax.dot_general(
            keys_ref[w * 32 : w * 32 + 32, g * 256 : g * 256 + 256],
            masked_heads(queries[w * 32 : w * 32 + 32, g * 256 : g * 256 + 256], 64, 4),
            NT,
            preferred_element_type=F32,
        )
        * scale
        + bias[g]
        for w, g in TWO_UNITS
    ]


def query_kernel(merged_ref, kv_ref, bias_ref, two_ref, two_sum_ref, query_out, score_out):
    merged = merged_ref[...]
    mean, factor = row_stats([merged.astype(F32)])
    total = jnp.dot(merged, two_ref[:, :512], preferred_element_type=F32)
    q = ((total - mean * two_sum_ref[0:1, :512]) * factor).astype(BF)
    query_out[...] = q
    for n, s in enumerate(scores_two(kv_ref, q, [bias_ref[g, 0:32] for g in range(2)])):
        score_out[n] = s


def level_two_kernel(
    query_ref, score_ref, kv_ref, other_ref, merged_ref, bias_ref, out_ref, two_out, result, sems
):
    far = scores_two(other_ref, query_ref[...], [bias_ref[g, 32:64] for g in range(2)])
    probs = [
        softmax_keys(jnp.concatenate([score_ref[n], s], axis=0), None).astype(BF)
        for n, s in enumerate(far)
    ]
    outs = []
    for p, (w, g) in zip(probs, TWO_UNITS):
        block = (slice(w * 32, w * 32 + 32), slice(512 + g * 256, 768 + g * 256))
        values = jnp.concatenate([kv_ref[block], other_ref[block]], axis=0)
        outs.append(lax.dot_general(p, values, TN, preferred_element_type=F32))
    picked = [pick_heads(o, 64, 4).astype(BF) for o in outs]
    attended = jnp.concatenate(
        [jnp.concatenate(picked[2 * w : 2 * w + 2], axis=1) for w in range(3)], axis=0
    )
    stores = []
    for part in range(2):
        lanes = slice(part * 512, part * 512 + 512)
        y = merged_ref[:, lanes].astype(F32) + jnp.dot(
            attended, out_ref[:, lanes], preferred_element_type=F32
        )
        for i in range(4):
            tiles = [y[32 * w + 8 * i : 32 * w + 8 * i + 8] for w in range(3)]
            result[i, :, lanes] = jnp.concatenate(tiles, axis=0).astype(BF)
        stores.append(
            pltpu.make_async_copy(result.at[:, :, lanes], two_out.at[:, :, lanes], sems.at[part])
        )
        stores[-1].start()
    for store in stores:
        store.wait()


def call(kernel, outs, args, hbm=0, scratch=(), mib=16, us=1.0, hbm_outs=0):
    shapes = [jax.ShapeDtypeStruct(s, d) for s, d in outs]
    place = [pl.BlockSpec(memory_space=pltpu.HBM)] * hbm
    place += [pl.BlockSpec(memory_space=pltpu.VMEM)] * (len(args) - hbm)
    args = [
        pltpu.with_memory_space_constraint(x, pltpu.HBM) if n < hbm else x
        for n, x in enumerate(args)
    ]
    return pl.pallas_call(
        kernel,
        out_shape=shapes,
        in_specs=place,
        out_specs=[pl.BlockSpec(memory_space=pltpu.HBM)] * hbm_outs
        + [pl.BlockSpec(memory_space=pltpu.VMEM)] * (len(outs) - hbm_outs),
        scratch_shapes=list(scratch),
        compiler_params=pltpu.CompilerParams(vmem_limit_bytes=mib * MIB),
        cost_estimate=pl.CostEstimate(
            flops=int(us * 10**9), bytes_accessed=10**6, transcendentals=0
        ),
        name=kernel.__name__,
    )(*args)


def on_device(
    tokens, region_ids, bias_one, qkv_one, out_one, merge_proj, bias_two, qkv_two, out_two
):
    lats, lons = lax.axis_size("lat"), lax.axis_size("lon")
    lat_inner = [(i, i ^ 1) for i in range(lats)]
    lat_outer = [(i, (i + (1 if i % 2 else -1)) % lats) for i in range(lats)]
    lon_inner = [(i, i ^ 1) for i in range(lons)]
    lon_outer = [(i, (i + (1 if i % 2 else -1)) % lons) for i in range(lons)]

    pair = lax.ppermute(tokens, "lat", lat_inner)
    pair_ids = lax.ppermute(region_ids, "lat", lat_inner)
    cross, tokens, region_ids = call(
        load_kernel,
        [((200, D1), BF), ((ROWS, COLS, D1), BF), ((ROWS, COLS), jnp.int32)],
        [tokens, region_ids],
        hbm=2,
        scratch=[pltpu.SemaphoreType.DMA((2,))],
        mib=4,
        us=4.0,
    )
    cross = lax.ppermute(cross, "lat", lat_outer)
    inside, own_edge, table_one, table_side, table_two = call(
        own_kernel,
        [
            ((2, INSIDE, 32, 3 * D1), BF), ((64, 3 * D1), BF), ((2, 4, 64, 128), F32),
            ((2, 2, 2, 64, 128), F32), ((2, 64, 128), F32),
        ],
        [qkv_one, bias_one, bias_two, tokens],
        scratch=[pltpu.VMEM((2, INSIDE, 2, 16, D1), BF)],
        us=1.5,
    )
    half_shape = pltpu.VMEM((INSIDE, 2, 16, D1), BF)
    pair_add, pair_edge = call(
        pair_kernel,
        [((INSIDE * 32, D1), F32), ((32, 2 * D1), BF)],
        [pair, pair_ids, region_ids, inside, qkv_one, table_one, out_one],
        scratch=[half_shape],
        us=0.3,
    )
    inner, outer, ids = call(
        edge_kernel,
        [((72, D1), BF), ((72, D1), BF), ((2 * ROWS, 128), F32)],
        [tokens, region_ids, pair, pair_ids, cross, pair_add],
        mib=4,
    )
    inner = lax.ppermute(inner, "lon", lon_inner)
    outer = lax.ppermute(outer, "lon", lon_outer)
    cross_add, cross_edge = call(
        cross_kernel,
        [((INSIDE * 32, D1), F32), ((32, 2 * D1), BF)],
        [cross, ids, inside, qkv_one, table_one, out_one],
        scratch=[half_shape],
        us=0.3,
    )
    merge_sum, two_sum = call(
        sums_kernel,
        [((8, D2), F32), ((8, 1536), F32)],
        [merge_proj, qkv_two, cross_edge],
        us=0.3,
    )
    level_one, merged, kv = call(
        final_kernel,
        [((ROWS, COLS, D1), BF), ((96, D2), BF), ((96, 1024), BF)],
        [
            tokens, inner, outer, ids, qkv_one, table_side, out_one, own_edge, pair_edge,
            cross_edge, pair_add, cross_add, merge_proj, qkv_two, merge_sum, two_sum,
        ],
        scratch=[
            pltpu.VMEM((4, ROWS, COLS, 128), F32),
            pltpu.VMEM((4, 3, 4, 8, D1), F32),
            pltpu.VMEM((ROWS, COLS, D1), BF),
            pltpu.SemaphoreType.DMA,
        ],
        hbm_outs=1,
    )
    other_kv = lax.ppermute(kv, "lat", lat_inner)
    query, scores = call(
        query_kernel,
        [((96, 512), BF), ((6, 32, 128), F32)],
        [merged, kv, table_two, qkv_two, two_sum],
    )
    (level_two,) = call(
        level_two_kernel,
        [((4, 24, D2), BF)],
        [query, scores, kv, other_kv, merged, table_two, out_two],
        scratch=[pltpu.VMEM((4, 24, D2), BF), pltpu.SemaphoreType.DMA((2,))],
        hbm_outs=1,
    )
    return (level_one, level_two)


def solution(mesh):
    placed = (P("lat", "lon", None), P("lat", "lon"), P(), P(), P(), P(), P(), P(), P())
    return jax.shard_map(
        on_device,
        mesh=mesh,
        in_specs=placed,
        out_specs=(P("lat", "lon", None), P("lat", "lon", None)),
        check_vma=False,
    )
```

```python
import math

import jax
import jax.numpy as jnp
from jax import lax
from jax.experimental import pallas as pl
from jax.experimental.pallas import tpu as pltpu
from jax.sharding import PartitionSpec as P

EPSILON = 1e-05
LOG2E = math.log2(math.e)
BF = jnp.bfloat16
F32 = jnp.float32
ROWS = 8
COLS = 48
TILES = 7
INSIDE = 5
FRAME = 56
D1 = 512
D2 = 1024
MIB = 1024 * 1024

NT = (((1,), (1,)), ((), ()))
TN = (((0,), (0,)), ((), ()))


def layer_norm(x):
    width = x.shape[-1]
    mean = jnp.sum(x, axis=-1, keepdims=True) * (1.0 / width)
    c = x - mean
    var = jnp.sum(c * c, axis=-1, keepdims=True) * (1.0 / width)
    return c * lax.rsqrt(var + EPSILON)


def row_stats(blocks):
    width = sum(x.shape[-1] for x in blocks)
    mean = sum(jnp.sum(x, axis=-1, keepdims=True) for x in blocks) * (1.0 / width)
    centered = [x - mean for x in blocks]
    var = sum(jnp.sum(c * c, axis=-1, keepdims=True) for c in centered) * (1.0 / width)
    return mean, lax.rsqrt(var + EPSILON)


def with_ones(x):
    return jnp.concatenate([x, jnp.ones((16, x.shape[1]), x.dtype)], axis=0)


def after_norm(total, mean, factor):
    count = mean.shape[0]
    return (total[0:count] - mean * total[count : count + 1]) * factor


def lanes_to(x, width):
    return jnp.concatenate([x, jnp.zeros((x.shape[0], width - x.shape[1]), x.dtype)], axis=1)


def lat_parity():
    return lax.rem(lax.axis_index("lat"), 2)


def lon_parity():
    return lax.rem(lax.axis_index("lon"), 2)


def start_all(pairs, sems):
    copies = [pltpu.make_async_copy(src, dst, sems.at[n]) for n, (src, dst) in enumerate(pairs)]
    for copy in copies:
        copy.start()
    return copies


def load_kernel(tok_hbm, ids_hbm, cross_ref, pair_ref, tok_ref, ids_ref, sems):
    copies = start_all([(ids_hbm, ids_ref), (tok_hbm, tok_ref)], sems)
    copies[0].wait()
    upper = lanes_to(ids_ref[...].astype(F32), D1)
    lower = pltpu.roll(upper, 4, 0)
    even = lat_parity() == 0
    cross_ref[4 * COLS :] = jnp.where(even, upper, lower).astype(BF)
    pair_ref[4 * COLS :] = jnp.where(even, lower, upper).astype(BF)
    copies[1].wait()
    for r in range(4):
        cross_ref[r * COLS : (r + 1) * COLS] = tok_ref[4 * lat_parity() + r]
        pair_ref[r * COLS : (r + 1) * COLS] = tok_ref[4 - 4 * lat_parity() + r]


def edge_kernel(
    tok_ref, ids_ref, pair_ref, cross_ref, after_ref, inner_ref, outer_ref, all_ids_ref
):
    first = [tok_ref[r, 0:16].astype(F32)[0:4] for r in range(ROWS)]
    first += [pair_ref[COLS * r : COLS * r + 16].astype(F32)[0:4] for r in range(4)]
    first += [cross_ref[COLS * r : COLS * r + 16].astype(F32)[0:4] for r in range(4)]
    last = [tok_ref[r, 32:48].astype(F32)[12:16] for r in range(ROWS)]
    last += [pair_ref[COLS * r + 32 : COLS * r + 48].astype(F32)[12:16] for r in range(4)]
    last += [cross_ref[COLS * r + 32 : COLS * r + 48].astype(F32)[12:16] for r in range(4)]
    own = lanes_to(ids_ref[...].astype(F32), 128)
    pair = pair_ref[4 * COLS :, 0:128].astype(F32)
    cross = cross_ref[4 * COLS :, 0:128].astype(F32)
    halo = jnp.concatenate([pair[0:4], cross[0:4]], axis=0)
    all_ids_ref[...] = jnp.concatenate([own, halo], axis=0)
    ids = jnp.concatenate([own, halo], axis=1)
    first = jnp.concatenate(first + [lanes_to(ids, D1)], axis=0).astype(BF)
    ids = pltpu.roll(ids, 256 - (COLS - 4), 1)
    last = jnp.concatenate(last + [lanes_to(ids, D1)], axis=0).astype(BF)
    even = lon_parity() == 0
    inner_ref[...] = jnp.where(even, last, first)
    outer_ref[...] = jnp.where(even, first, last)


def sides(inner_ref, outer_ref):
    inner, outer = inner_ref[...].astype(F32), outer_ref[...].astype(F32)
    even = lon_parity() == 0
    return jnp.where(even, outer, inner), jnp.where(even, inner, outer)


def side_pieces(x, row):
    order = [row + r for r in range(4)] + [4 - row + r for r in range(4)]
    west = [x[8 * r + c : 8 * r + c + 4] for c in (4, 0) for r in order]
    east = [x[8 * r + c : 8 * r + c + 4] for c in (0, 4) for r in order]
    return west, east


def own_kernel(
    qkv_ref, one_ref, two_ref, tok_ref, inside_out, edge_out, one_out, side_out, two_out, normed
):
    first, last = [], []
    for r in range(0, ROWS, 2):
        pair = []
        for k in range(2):
            x = layer_norm(tok_ref[r + k].astype(F32))
            pair.append(x[4 : COLS - 4].reshape(INSIDE, 8, D1))
            first.append(x[0:4])
            last.append(x[COLS - 4 :])
        normed[r // 4, :, (r % 4) // 2] = jnp.concatenate(pair, axis=1).astype(BF)
    edge = jnp.concatenate(first[0:4] + last[0:4] + first[4:8] + last[4:8], axis=0).astype(BF)
    for half in range(2):
        low = 32 * (1 - half)
        for g in range(4):
            turned = one_ref[4 * g : 4 * g + 4, low : low + 32, :].reshape(128, 64).T * LOG2E
            one_out[half, g, 0:32] = turned[low : low + 32]
            one_out[half, g, 32:64] = turned[32 - low : 64 - low]
    for half in range(2):
        row = 4 * (1 - half)
        for g in range(2):
            heads = [side_pieces(one_ref[8 * g + h], row) for h in range(8)]
            for side in range(2):
                part = jnp.concatenate([x for h in heads for x in h[side][0:4]], axis=0)
                pieces = side_pieces(part.T * LOG2E, row)[side]
                side_out[half, side, g] = jnp.concatenate(pieces, axis=0)
    low = pl.multiple_of(lat_parity() * 32, 32)
    for g in range(2):
        turned = two_ref[4 * g : 4 * g + 4, pl.ds(low, 32), :].reshape(128, 64).T * LOG2E
        even = lat_parity() == 0
        two_out[g, 0:32] = jnp.where(even, turned[0:32], turned[32:64])
        two_out[g, 32:64] = jnp.where(even, turned[32:64], turned[0:32])
    x = jnp.concatenate([normed[...].reshape(2 * INSIDE * 32, D1), edge], axis=0)
    qkv = jnp.dot(x, qkv_ref[...], preferred_element_type=F32).astype(BF)
    inside_out[...] = qkv[0 : 2 * INSIDE * 32].reshape(2, INSIDE, 32, 3 * D1)
    edge_out[...] = qkv[2 * INSIDE * 32 :]


def masked_heads(q, head_dim, count):
    lane = lax.broadcasted_iota(jnp.int32, q.shape, 1) // head_dim
    zero = jnp.zeros_like(q)
    return jnp.concatenate([jnp.where(lane == h, q, zero) for h in range(count)], axis=0)


def pick_heads(o, head_dim, count):
    rows = o.shape[0] // count
    lane = lax.broadcasted_iota(jnp.int32, (rows, o.shape[1]), 1) // head_dim
    out = o[0:rows]
    for h in range(1, count):
        out = jnp.where(lane == h, o[h * rows : (h + 1) * rows], out)
    return out


def softmax_keys(s, allowed):
    if allowed is not None:
        s = jnp.where(allowed, s, -1e30)
    p = jnp.exp2(s - jnp.max(s, axis=0, keepdims=True))
    return p * (1.0 / jnp.sum(p, axis=0, keepdims=True))


def region_masks(own, halo):
    turned = jnp.concatenate([own, halo, jnp.zeros((120, 128), F32)], axis=0).T

    def window(j):
        tiles = [
            jnp.broadcast_to(turned[8 * j : 8 * j + 8, r : r + 1], (8, 128)) for r in range(8)
        ]
        queries = jnp.concatenate(tiles[0:4] * 4, axis=0).T[0:1]
        return jnp.concatenate(tiles, axis=0) == queries

    return window


def in_range(cross_ids):
    lat = lax.axis_index("lat")
    outside = (lat == 0) | (lat == lax.axis_size("lat") - 1)
    return jnp.where(outside, -1.0, cross_ids)


def attend_one(halves, allowed, bias_ref, query, keys, values):
    scale = LOG2E / math.sqrt(32)
    units = [(w, g) for w in range(len(halves)) for g in range(4)]
    scores = [
        lax.dot_general(
            keys(w, g), masked_heads(query(w, g), 32, 4), NT, preferred_element_type=F32
        )
        for w, g in units
    ]
    probs = [
        softmax_keys(s * scale + bias_ref[halves[w], g], allowed[w]).astype(BF)
        for s, (w, g) in zip(scores, units)
    ]
    outs = [
        lax.dot_general(p, values(w, g), TN, preferred_element_type=F32)
        for p, (w, g) in zip(probs, units)
    ]
    picked = [pick_heads(o, 32, 4).astype(BF) for o in outs]
    return [jnp.concatenate(picked[4 * w : 4 * w + 4], axis=1) for w in range(len(halves))]


def lanes_of(block, g):
    return slice(block * D1 + g * 128, block * D1 + g * 128 + 128)


def half_inner(half, halo_rows, own_ids, halo_ids, inside_ref, qkv_ref, bias_ref, out_ref, normed):
    rows = [layer_norm(x) for x in halo_rows]
    for r in range(0, 4, 2):
        pair = [rows[k][4 : COLS - 4].reshape(INSIDE, 8, D1) for k in (r, r + 1)]
        normed[:, r // 2] = jnp.concatenate(pair, axis=1).astype(BF)
    edge = jnp.concatenate([x[0:4] for x in rows] + [x[COLS - 4 :] for x in rows], axis=0)
    halo = jnp.dot(
        jnp.concatenate([normed[...].reshape(INSIDE * 32, D1), edge.astype(BF)], axis=0),
        qkv_ref[:, D1:],
        preferred_element_type=F32,
    ).astype(BF)
    mask = region_masks(pltpu.roll(own_ids, 4, 1), pltpu.roll(halo_ids, 4, 1))

    def both(w, block, g):
        own = inside_ref[half, w, :, lanes_of(block, g)]
        return jnp.concatenate([own, halo[32 * w : 32 * w + 32, lanes_of(block - 1, g)]], axis=0)

    attended = attend_one(
        [half] * INSIDE,
        [mask(j) for j in range(1, TILES - 1)],
        bias_ref,
        lambda w, g: inside_ref[half, w, :, lanes_of(0, g)],
        lambda w, g: both(w, 1, g),
        lambda w, g: both(w, 2, g),
    )
    add = jnp.dot(jnp.concatenate(attended, axis=0), out_ref[...], preferred_element_type=F32)
    return add, halo[INSIDE * 32 :]


def pair_kernel(
    pair_ref, ids_ref, inside_ref, qkv_ref, bias_ref, out_ref, add_out, edge_out, normed
):
    even = lat_parity() == 0
    own = lanes_to(ids_ref[...].astype(F32), 128)
    pair = pair_ref[4 * COLS :, 0:128].astype(F32)
    own = jnp.where(even, pltpu.roll(own, 4, 0), own)
    rows = [pair_ref[COLS * r : COLS * r + COLS].astype(F32) for r in range(4)]
    add_out[...], edge_out[...] = half_inner(
        1 - lat_parity(), rows, own[0:4], pair[0:4], inside_ref, qkv_ref, bias_ref, out_ref, normed
    )


def cross_kernel(
    cross_ref, ids_ref, inside_ref, qkv_ref, bias_ref, out_ref, add_out, edge_out, normed
):
    ids = ids_ref[...]
    own = jnp.where(lat_parity() == 0, ids[0:4], ids[4:8])
    rows = [cross_ref[COLS * r : COLS * r + COLS].astype(F32) for r in range(4)]
    add_out[...], edge_out[...] = half_inner(
        lat_parity(), rows, own, in_range(ids[12:16]), inside_ref, qkv_ref, bias_ref, out_ref, normed
    )


def final_kernel(
    tok_ref, inner_ref, outer_ref, ids_ref, qkv_ref, bias_ref, out_ref, own_edge_ref,
    pair_edge_ref, cross_edge_ref, pair_add_ref, cross_add_ref, merge_ref, two_ref,
    one_out, merged_out, kv_out,
    level, parts, done, sem,
):
    even = lat_parity() == 0
    west, east = sides(inner_ref, outer_ref)
    x = layer_norm(jnp.concatenate([west[0:64], east[0:64]], axis=0)).astype(BF)
    new = jnp.dot(x, qkv_ref[:, D1:], preferred_element_type=F32).astype(BF)

    lane = lax.broadcasted_iota(jnp.int32, (2 * ROWS, 128), 1)
    own = pltpu.roll(ids_ref[...], 4, 1)
    near = jnp.concatenate([west[64:72, 0:128], west[64:72, 128:256]], axis=0)
    far = jnp.concatenate([east[64:72, 0:128], east[64:72, 128:256]], axis=0)
    far = pltpu.roll(far, COLS + 4, 1)
    ids = jnp.where(lane < 4, near, jnp.where(lane < COLS + 4, own, far))
    pair_ids, cross_ids = ids[8:12], in_range(ids[12:16])
    above, below = jnp.where(even, cross_ids, pair_ids), jnp.where(even, pair_ids, cross_ids)
    rows = [ids[0:4], above, ids[4:8], below, jnp.zeros((112, 128), F32)]
    turned = jnp.concatenate(rows, axis=0).T

    windows = [(half, side) for half in range(2) for side in range(2)]
    keys, values, queries, allowed = [], [], [], []
    for half, side in windows:
        at = 16 * (2 * half + side)
        a, b = cross_edge_ref, pair_edge_ref
        c, d = new[64 * side + 48 : 64 * side + 64], new[64 * side + 32 : 64 * side + 48]
        if half == 1:
            a, b, c, d = b, a, d, c
        lines = slice(16 * side, 16 * side + 16)
        kv = jnp.concatenate(
            [
                own_edge_ref[at : at + 16, D1:],
                jnp.where(even, a[lines], b[lines]),
                new[64 * side + 16 * half : 64 * side + 16 * half + 16],
                jnp.where(even, c, d),
            ],
            axis=0,
        )
        keys.append(kv[:, 0:D1])
        values.append(kv[:, D1:])
        queries.append(own_edge_ref[at : at + 16, 0:D1])
        starts = (4, 0) if side == 0 else (COLS, COLS + 4)
        pieces = [
            jnp.broadcast_to(turned[c0 : c0 + 4, r : r + 1], (4, 128))
            for c0 in starts
            for r in range(8 * half, 8 * half + 8)
        ]
        own_ids = jnp.concatenate(pieces[0:4] * 8, axis=0).T[0:1]
        allowed.append(jnp.concatenate(pieces, axis=0) == own_ids)
    scale = LOG2E / math.sqrt(32)
    units = [(w, g) for w in range(4) for g in range(2)]
    scores = [
        lax.dot_general(
            keys[w][:, 256 * g : 256 * g + 256],
            masked_heads(queries[w][:, 256 * g : 256 * g + 256], 32, 8),
            NT,
            preferred_element_type=F32,
        )
        for w, g in units
    ]
    probs = [
        softmax_keys(s * scale + bias_ref[windows[w][0], windows[w][1], g], allowed[w]).astype(BF)
        for s, (w, g) in zip(scores, units)
    ]
    outs = [
        lax.dot_general(p, values[w][:, 256 * g : 256 * g + 256], TN, preferred_element_type=F32)
        for p, (w, g) in zip(probs, units)
    ]
    picked = [pick_heads(o, 32, 8).astype(BF) for o in outs]
    attended = [jnp.concatenate(picked[2 * w : 2 * w + 2], axis=1) for w in range(4)]
    edge = jnp.dot(jnp.concatenate(attended, axis=0), out_ref[...], preferred_element_type=F32)
    for row in range(ROWS):
        half, r = row // 4, row % 4
        at = 32 * half + 4 * r
        adds = [edge[at : at + 4]]
        for j in range(INSIDE):
            tile = slice(32 * j + 8 * r, 32 * j + 8 * r + 8)
            upper, lower = cross_add_ref[tile], pair_add_ref[tile]
            if half == 1:
                upper, lower = lower, upper
            adds.append(jnp.where(even, upper, lower))
        adds.append(edge[at + 16 : at + 20])
        value = (tok_ref[row].astype(F32) + jnp.concatenate(adds, axis=0)).astype(BF)
        done[row] = value
        for n in range(4):
            level[n, row] = value[:, n * 128 : n * 128 + 128].astype(F32)
    store = pltpu.make_async_copy(done, one_out, sem)
    store.start()

    means, factors = [], []
    for i in range(4):
        quartet = [
            jnp.concatenate(
                [level[n, 2 * i + dr, pl.ds(dc, COLS // 2, 2), :] for n in range(4)], axis=1
            )
            for dc in range(2)
            for dr in range(2)
        ]
        for n in range(4):
            parts[n, :, i] = quartet[n].reshape(3, 8, D1)
        mean, factor = row_stats(quartet)
        means.append(mean)
        factors.append(factor)
    order = [(i, slice(8 * w, 8 * w + 8)) for w in range(3) for i in range(4)]
    mean = jnp.concatenate([means[i][at] for i, at in order], axis=0)
    factor = jnp.concatenate([factors[i][at] for i, at in order], axis=0)
    total = jnp.zeros((112, D2), F32)
    for n in range(4):
        total += jnp.dot(
            with_ones(parts[n].reshape(96, D1).astype(BF)),
            merge_ref[n * D1 : (n + 1) * D1, :],
            preferred_element_type=F32,
        )
    merged = after_norm(total, mean, factor).astype(BF)
    merged_out[...] = merged
    mean, factor = row_stats([merged.astype(F32)])
    total = jnp.dot(with_ones(merged), two_ref[:, 512:], preferred_element_type=F32)
    kv_out[...] = after_norm(total, mean, factor).astype(BF)
    store.wait()


TWO_UNITS = [(w, g) for w in range(3) for g in range(2)]


def scores_two(keys_ref, queries, bias):
    scale = LOG2E / math.sqrt(64)
    return [
        lax.dot_general(
            keys_ref[w * 32 : w * 32 + 32, g * 256 : g * 256 + 256],
            masked_heads(queries[w * 32 : w * 32 + 32, g * 256 : g * 256 + 256], 64, 4),
            NT,
            preferred_element_type=F32,
        )
        * scale
        + bias[g]
        for w, g in TWO_UNITS
    ]


def query_kernel(merged_ref, kv_ref, bias_ref, two_ref, query_out, score_out):
    merged = merged_ref[...]
    mean, factor = row_stats([merged.astype(F32)])
    total = jnp.dot(with_ones(merged), two_ref[:, :512], preferred_element_type=F32)
    q = after_norm(total, mean, factor).astype(BF)
    query_out[...] = q
    for n, s in enumerate(scores_two(kv_ref, q, [bias_ref[g, 0:32] for g in range(2)])):
        score_out[n] = s


def level_two_kernel(
    query_ref, score_ref, kv_ref, other_ref, merged_ref, bias_ref, out_ref, two_out, result, sems
):
    far = scores_two(other_ref, query_ref[...], [bias_ref[g, 32:64] for g in range(2)])
    probs = [
        softmax_keys(jnp.concatenate([score_ref[n], s], axis=0), None).astype(BF)
        for n, s in enumerate(far)
    ]
    outs = []
    for p, (w, g) in zip(probs, TWO_UNITS):
        block = (slice(w * 32, w * 32 + 32), slice(512 + g * 256, 768 + g * 256))
        values = jnp.concatenate([kv_ref[block], other_ref[block]], axis=0)
        outs.append(lax.dot_general(p, values, TN, preferred_element_type=F32))
    picked = [pick_heads(o, 64, 4).astype(BF) for o in outs]
    attended = jnp.concatenate(
        [jnp.concatenate(picked[2 * w : 2 * w + 2], axis=1) for w in range(3)], axis=0
    )
    stores = []
    for part in range(2):
        lanes = slice(part * 512, part * 512 + 512)
        y = merged_ref[:, lanes].astype(F32) + jnp.dot(
            attended, out_ref[:, lanes], preferred_element_type=F32
        )
        for i in range(4):
            tiles = [y[32 * w + 8 * i : 32 * w + 8 * i + 8] for w in range(3)]
            result[i, :, lanes] = jnp.concatenate(tiles, axis=0).astype(BF)
        stores.append(
            pltpu.make_async_copy(result.at[:, :, lanes], two_out.at[:, :, lanes], sems.at[part])
        )
        stores[-1].start()
    for store in stores:
        store.wait()


def call(kernel, outs, args, hbm=0, scratch=(), mib=16, us=1.0, hbm_outs=0):
    shapes = [jax.ShapeDtypeStruct(s, d) for s, d in outs]
    place = [pl.BlockSpec(memory_space=pltpu.HBM)] * hbm
    place += [pl.BlockSpec(memory_space=pltpu.VMEM)] * (len(args) - hbm)
    args = [
        pltpu.with_memory_space_constraint(x, pltpu.HBM) if n < hbm else x
        for n, x in enumerate(args)
    ]
    return pl.pallas_call(
        kernel,
        out_shape=shapes,
        in_specs=place,
        out_specs=[pl.BlockSpec(memory_space=pltpu.HBM)] * hbm_outs
        + [pl.BlockSpec(memory_space=pltpu.VMEM)] * (len(outs) - hbm_outs),
        scratch_shapes=list(scratch),
        compiler_params=pltpu.CompilerParams(vmem_limit_bytes=mib * MIB),
        cost_estimate=pl.CostEstimate(
            flops=int(us * 10**9), bytes_accessed=10**6, transcendentals=0
        ),
        name=kernel.__name__,
    )(*args)


def on_device(
    tokens, region_ids, bias_one, qkv_one, out_one, merge_proj, bias_two, qkv_two, out_two
):
    lats, lons = lax.axis_size("lat"), lax.axis_size("lon")
    lat_inner = [(i, i ^ 1) for i in range(lats)]
    lat_outer = [(i, (i + (1 if i % 2 else -1)) % lats) for i in range(lats)]
    lon_inner = [(i, i ^ 1) for i in range(lons)]
    lon_outer = [(i, (i + (1 if i % 2 else -1)) % lons) for i in range(lons)]

    cross, pair, tokens, region_ids = call(
        load_kernel,
        [((200, D1), BF), ((200, D1), BF), ((ROWS, COLS, D1), BF), ((ROWS, COLS), jnp.int32)],
        [tokens, region_ids],
        hbm=2,
        scratch=[pltpu.SemaphoreType.DMA((2,))],
        mib=4,
        us=4.0,
    )
    cross = lax.ppermute(cross, "lat", lat_outer)
    pair = lax.ppermute(pair, "lat", lat_inner)
    inside, own_edge, table_one, table_side, table_two = call(
        own_kernel,
        [
            ((2, INSIDE, 32, 3 * D1), BF), ((64, 3 * D1), BF), ((2, 4, 64, 128), F32),
            ((2, 2, 2, 64, 128), F32), ((2, 64, 128), F32),
        ],
        [qkv_one, bias_one, bias_two, tokens],
        scratch=[pltpu.VMEM((2, INSIDE, 2, 16, D1), BF)],
        us=1.5,
    )
    half_shape = pltpu.VMEM((INSIDE, 2, 16, D1), BF)
    pair_add, pair_edge = call(
        pair_kernel,
        [((INSIDE * 32, D1), F32), ((32, 2 * D1), BF)],
        [pair, region_ids, inside, qkv_one, table_one, out_one],
        scratch=[half_shape],
        us=0.3,
    )
    inner, outer, ids = call(
        edge_kernel,
        [((72, D1), BF), ((72, D1), BF), ((2 * ROWS, 128), F32)],
        [tokens, region_ids, pair, cross, pair_add],
        mib=4,
    )
    inner = lax.ppermute(inner, "lon", lon_inner)
    outer = lax.ppermute(outer, "lon", lon_outer)
    cross_add, cross_edge = call(
        cross_kernel,
        [((INSIDE * 32, D1), F32), ((32, 2 * D1), BF)],
        [cross, ids, inside, qkv_one, table_one, out_one],
        scratch=[half_shape],
        us=0.3,
    )
    level_one, merged, kv = call(
        final_kernel,
        [((ROWS, COLS, D1), BF), ((96, D2), BF), ((96, 1024), BF)],
        [
            tokens, inner, outer, ids, qkv_one, table_side, out_one, own_edge, pair_edge,
            cross_edge, pair_add, cross_add, merge_proj, qkv_two,
        ],
        scratch=[
            pltpu.VMEM((4, ROWS, COLS, 128), F32),
            pltpu.VMEM((4, 3, 4, 8, D1), F32),
            pltpu.VMEM((ROWS, COLS, D1), BF),
            pltpu.SemaphoreType.DMA,
        ],
        hbm_outs=1,
    )
    other_kv = lax.ppermute(kv, "lat", lat_inner)
    query, scores = call(
        query_kernel,
        [((96, 512), BF), ((6, 32, 128), F32)],
        [merged, kv, table_two, qkv_two],
    )
    (level_two,) = call(
        level_two_kernel,
        [((4, 24, D2), BF)],
        [query, scores, kv, other_kv, merged, table_two, out_two],
        scratch=[pltpu.VMEM((4, 24, D2), BF), pltpu.SemaphoreType.DMA((2,))],
        hbm_outs=1,
    )
    return (level_one, level_two)


def solution(mesh):
    placed = (P("lat", "lon", None), P("lat", "lon"), P(), P(), P(), P(), P(), P(), P())
    return jax.shard_map(
        on_device,
        mesh=mesh,
        in_specs=placed,
        out_specs=(P("lat", "lon", None), P("lat", "lon", None)),
        check_vma=False,
    )
```

```python
import math

import jax
import jax.numpy as jnp
from jax import lax
from jax.experimental import pallas as pl
from jax.experimental.pallas import tpu as pltpu
from jax.sharding import PartitionSpec as P

EPSILON = 1e-05
LOG2E = math.log2(math.e)
BF = jnp.bfloat16
F32 = jnp.float32
ROWS = 8
COLS = 48
TILES = 7
INSIDE = 5
FRAME = 56
D1 = 512
D2 = 1024
MIB = 1024 * 1024

NT = (((1,), (1,)), ((), ()))
TN = (((0,), (0,)), ((), ()))


def layer_norm(x):
    width = x.shape[-1]
    mean = jnp.sum(x, axis=-1, keepdims=True) * (1.0 / width)
    c = x - mean
    var = jnp.sum(c * c, axis=-1, keepdims=True) * (1.0 / width)
    return c * lax.rsqrt(var + EPSILON)


def row_stats(blocks):
    width = sum(x.shape[-1] for x in blocks)
    mean = sum(jnp.sum(x, axis=-1, keepdims=True) for x in blocks) * (1.0 / width)
    centered = [x - mean for x in blocks]
    var = sum(jnp.sum(c * c, axis=-1, keepdims=True) for c in centered) * (1.0 / width)
    return mean, lax.rsqrt(var + EPSILON)


def with_ones(x):
    return jnp.concatenate([x, jnp.ones((16, x.shape[1]), x.dtype)], axis=0)


def after_norm(total, mean, factor):
    count = mean.shape[0]
    return (total[0:count] - mean * total[count : count + 1]) * factor


def lanes_to(x, width):
    return jnp.concatenate([x, jnp.zeros((x.shape[0], width - x.shape[1]), x.dtype)], axis=1)


def lat_parity():
    return lax.rem(lax.axis_index("lat"), 2)


def lon_parity():
    return lax.rem(lax.axis_index("lon"), 2)


def start_all(pairs, sems):
    copies = [pltpu.make_async_copy(src, dst, sems.at[n]) for n, (src, dst) in enumerate(pairs)]
    for copy in copies:
        copy.start()
    return copies


def load_kernel(tok_hbm, ids_hbm, cross_ref, pair_ref, ids_ref, sems):
    copies = [(ids_hbm, ids_ref)]
    for r in range(4):
        row = slice(r * COLS, (r + 1) * COLS)
        copies.append((tok_hbm.at[4 * lat_parity() + r], cross_ref.at[row]))
        copies.append((tok_hbm.at[4 - 4 * lat_parity() + r], pair_ref.at[row]))
    copies = start_all(copies, sems)
    copies[0].wait()
    upper = lanes_to(ids_ref[...].astype(F32), D1)
    lower = pltpu.roll(upper, 4, 0)
    even = lat_parity() == 0
    cross_ref[4 * COLS :] = jnp.where(even, upper, lower).astype(BF)
    pair_ref[4 * COLS :] = jnp.where(even, lower, upper).astype(BF)
    for copy in copies[1:]:
        copy.wait()


def edge_kernel(
    tok_ref, ids_ref, pair_ref, cross_ref, after_ref, inner_ref, outer_ref, all_ids_ref
):
    first = [tok_ref[r, 0:16].astype(F32)[0:4] for r in range(ROWS)]
    first += [pair_ref[COLS * r : COLS * r + 16].astype(F32)[0:4] for r in range(4)]
    first += [cross_ref[COLS * r : COLS * r + 16].astype(F32)[0:4] for r in range(4)]
    last = [tok_ref[r, 32:48].astype(F32)[12:16] for r in range(ROWS)]
    last += [pair_ref[COLS * r + 32 : COLS * r + 48].astype(F32)[12:16] for r in range(4)]
    last += [cross_ref[COLS * r + 32 : COLS * r + 48].astype(F32)[12:16] for r in range(4)]
    own = lanes_to(ids_ref[...].astype(F32), 128)
    pair = pair_ref[4 * COLS :, 0:128].astype(F32)
    cross = cross_ref[4 * COLS :, 0:128].astype(F32)
    halo = jnp.concatenate([pair[0:4], cross[0:4]], axis=0)
    all_ids_ref[...] = jnp.concatenate([own, halo], axis=0)
    ids = jnp.concatenate([own, halo], axis=1)
    first = jnp.concatenate(first + [lanes_to(ids, D1)], axis=0).astype(BF)
    ids = pltpu.roll(ids, 256 - (COLS - 4), 1)
    last = jnp.concatenate(last + [lanes_to(ids, D1)], axis=0).astype(BF)
    even = lon_parity() == 0
    inner_ref[...] = jnp.where(even, last, first)
    outer_ref[...] = jnp.where(even, first, last)


def sides(inner_ref, outer_ref):
    inner, outer = inner_ref[...].astype(F32), outer_ref[...].astype(F32)
    even = lon_parity() == 0
    return jnp.where(even, outer, inner), jnp.where(even, inner, outer)


def side_pieces(x, row):
    order = [row + r for r in range(4)] + [4 - row + r for r in range(4)]
    west = [x[8 * r + c : 8 * r + c + 4] for c in (4, 0) for r in order]
    east = [x[8 * r + c : 8 * r + c + 4] for c in (0, 4) for r in order]
    return west, east


def own_kernel(
    qkv_ref, one_ref, two_ref, tok_ref, inside_out, edge_out, one_out, side_out, two_out, normed
):
    first, last = [], []
    for r in range(0, ROWS, 2):
        pair = []
        for k in range(2):
            x = layer_norm(tok_ref[r + k].astype(F32))
            pair.append(x[4 : COLS - 4].reshape(INSIDE, 8, D1))
            first.append(x[0:4])
            last.append(x[COLS - 4 :])
        normed[r // 4, :, (r % 4) // 2] = jnp.concatenate(pair, axis=1).astype(BF)
    edge = jnp.concatenate(first[0:4] + last[0:4] + first[4:8] + last[4:8], axis=0).astype(BF)
    for half in range(2):
        low = 32 * (1 - half)
        for g in range(4):
            turned = one_ref[4 * g : 4 * g + 4, low : low + 32, :].reshape(128, 64).T * LOG2E
            one_out[half, g, 0:32] = turned[low : low + 32]
            one_out[half, g, 32:64] = turned[32 - low : 64 - low]
    for half in range(2):
        row = 4 * (1 - half)
        for g in range(2):
            heads = [side_pieces(one_ref[8 * g + h], row) for h in range(8)]
            for side in range(2):
                part = jnp.concatenate([x for h in heads for x in h[side][0:4]], axis=0)
                pieces = side_pieces(part.T * LOG2E, row)[side]
                side_out[half, side, g] = jnp.concatenate(pieces, axis=0)
    low = pl.multiple_of(lat_parity() * 32, 32)
    for g in range(2):
        turned = two_ref[4 * g : 4 * g + 4, pl.ds(low, 32), :].reshape(128, 64).T * LOG2E
        even = lat_parity() == 0
        two_out[g, 0:32] = jnp.where(even, turned[0:32], turned[32:64])
        two_out[g, 32:64] = jnp.where(even, turned[32:64], turned[0:32])
    x = jnp.concatenate([normed[...].reshape(2 * INSIDE * 32, D1), edge], axis=0)
    qkv = jnp.dot(x, qkv_ref[...], preferred_element_type=F32).astype(BF)
    inside_out[...] = qkv[0 : 2 * INSIDE * 32].reshape(2, INSIDE, 32, 3 * D1)
    edge_out[...] = qkv[2 * INSIDE * 32 :]


def masked_heads(q, head_dim, count):
    lane = lax.broadcasted_iota(jnp.int32, q.shape, 1) // head_dim
    zero = jnp.zeros_like(q)
    return jnp.concatenate([jnp.where(lane == h, q, zero) for h in range(count)], axis=0)


def pick_heads(o, head_dim, count):
    rows = o.shape[0] // count
    lane = lax.broadcasted_iota(jnp.int32, (rows, o.shape[1]), 1) // head_dim
    out = o[0:rows]
    for h in range(1, count):
        out = jnp.where(lane == h, o[h * rows : (h + 1) * rows], out)
    return out


def softmax_keys(s, allowed):
    if allowed is not None:
        s = jnp.where(allowed, s, -1e30)
    p = jnp.exp2(s - jnp.max(s, axis=0, keepdims=True))
    return p * (1.0 / jnp.sum(p, axis=0, keepdims=True))


def region_masks(own, halo):
    turned = jnp.concatenate([own, halo, jnp.zeros((120, 128), F32)], axis=0).T

    def window(j):
        tiles = [
            jnp.broadcast_to(turned[8 * j : 8 * j + 8, r : r + 1], (8, 128)) for r in range(8)
        ]
        queries = jnp.concatenate(tiles[0:4] * 4, axis=0).T[0:1]
        return jnp.concatenate(tiles, axis=0) == queries

    return window


def in_range(cross_ids):
    lat = lax.axis_index("lat")
    outside = (lat == 0) | (lat == lax.axis_size("lat") - 1)
    return jnp.where(outside, -1.0, cross_ids)


def attend_one(halves, allowed, bias_ref, query, keys, values):
    scale = LOG2E / math.sqrt(32)
    units = [(w, g) for w in range(len(halves)) for g in range(4)]
    scores = [
        lax.dot_general(
            keys(w, g), masked_heads(query(w, g), 32, 4), NT, preferred_element_type=F32
        )
        for w, g in units
    ]
    probs = [
        softmax_keys(s * scale + bias_ref[halves[w], g], allowed[w]).astype(BF)
        for s, (w, g) in zip(scores, units)
    ]
    outs = [
        lax.dot_general(p, values(w, g), TN, preferred_element_type=F32)
        for p, (w, g) in zip(probs, units)
    ]
    picked = [pick_heads(o, 32, 4).astype(BF) for o in outs]
    return [jnp.concatenate(picked[4 * w : 4 * w + 4], axis=1) for w in range(len(halves))]


def lanes_of(block, g):
    return slice(block * D1 + g * 128, block * D1 + g * 128 + 128)


def half_inner(half, halo_rows, own_ids, halo_ids, inside_ref, qkv_ref, bias_ref, out_ref, normed):
    rows = [layer_norm(x) for x in halo_rows]
    for r in range(0, 4, 2):
        pair = [rows[k][4 : COLS - 4].reshape(INSIDE, 8, D1) for k in (r, r + 1)]
        normed[:, r // 2] = jnp.concatenate(pair, axis=1).astype(BF)
    edge = jnp.concatenate([x[0:4] for x in rows] + [x[COLS - 4 :] for x in rows], axis=0)
    halo = jnp.dot(
        jnp.concatenate([normed[...].reshape(INSIDE * 32, D1), edge.astype(BF)], axis=0),
        qkv_ref[:, D1:],
        preferred_element_type=F32,
    ).astype(BF)
    mask = region_masks(pltpu.roll(own_ids, 4, 1), pltpu.roll(halo_ids, 4, 1))

    def both(w, block, g):
        own = inside_ref[half, w, :, lanes_of(block, g)]
        return jnp.concatenate([own, halo[32 * w : 32 * w + 32, lanes_of(block - 1, g)]], axis=0)

    attended = attend_one(
        [half] * INSIDE,
        [mask(j) for j in range(1, TILES - 1)],
        bias_ref,
        lambda w, g: inside_ref[half, w, :, lanes_of(0, g)],
        lambda w, g: both(w, 1, g),
        lambda w, g: both(w, 2, g),
    )
    add = jnp.dot(jnp.concatenate(attended, axis=0), out_ref[...], preferred_element_type=F32)
    return add, halo[INSIDE * 32 :]


def pair_kernel(
    pair_ref, ids_ref, inside_ref, qkv_ref, bias_ref, out_ref, add_out, edge_out, normed
):
    even = lat_parity() == 0
    own = lanes_to(ids_ref[...].astype(F32), 128)
    pair = pair_ref[4 * COLS :, 0:128].astype(F32)
    own = jnp.where(even, pltpu.roll(own, 4, 0), own)
    rows = [pair_ref[COLS * r : COLS * r + COLS].astype(F32) for r in range(4)]
    add_out[...], edge_out[...] = half_inner(
        1 - lat_parity(), rows, own[0:4], pair[0:4], inside_ref, qkv_ref, bias_ref, out_ref, normed
    )


def cross_kernel(
    cross_ref, ids_ref, inside_ref, qkv_ref, bias_ref, out_ref, add_out, edge_out, normed
):
    ids = ids_ref[...]
    own = jnp.where(lat_parity() == 0, ids[0:4], ids[4:8])
    rows = [cross_ref[COLS * r : COLS * r + COLS].astype(F32) for r in range(4)]
    add_out[...], edge_out[...] = half_inner(
        lat_parity(), rows, own, in_range(ids[12:16]), inside_ref, qkv_ref, bias_ref, out_ref, normed
    )


def final_kernel(
    tok_ref, inner_ref, outer_ref, ids_ref, qkv_ref, bias_ref, out_ref, own_edge_ref,
    pair_edge_ref, cross_edge_ref, pair_add_ref, cross_add_ref, merge_ref, two_ref,
    one_out, merged_out, kv_out,
    level, parts, done, sem,
):
    even = lat_parity() == 0
    west, east = sides(inner_ref, outer_ref)
    x = layer_norm(jnp.concatenate([west[0:64], east[0:64]], axis=0)).astype(BF)
    new = jnp.dot(x, qkv_ref[:, D1:], preferred_element_type=F32).astype(BF)

    lane = lax.broadcasted_iota(jnp.int32, (2 * ROWS, 128), 1)
    own = pltpu.roll(ids_ref[...], 4, 1)
    near = jnp.concatenate([west[64:72, 0:128], west[64:72, 128:256]], axis=0)
    far = jnp.concatenate([east[64:72, 0:128], east[64:72, 128:256]], axis=0)
    far = pltpu.roll(far, COLS + 4, 1)
    ids = jnp.where(lane < 4, near, jnp.where(lane < COLS + 4, own, far))
    pair_ids, cross_ids = ids[8:12], in_range(ids[12:16])
    above, below = jnp.where(even, cross_ids, pair_ids), jnp.where(even, pair_ids, cross_ids)
    rows = [ids[0:4], above, ids[4:8], below, jnp.zeros((112, 128), F32)]
    turned = jnp.concatenate(rows, axis=0).T

    windows = [(half, side) for half in range(2) for side in range(2)]
    keys, values, queries, allowed = [], [], [], []
    for half, side in windows:
        at = 16 * (2 * half + side)
        a, b = cross_edge_ref, pair_edge_ref
        c, d = new[64 * side + 48 : 64 * side + 64], new[64 * side + 32 : 64 * side + 48]
        if half == 1:
            a, b, c, d = b, a, d, c
        lines = slice(16 * side, 16 * side + 16)
        kv = jnp.concatenate(
            [
                own_edge_ref[at : at + 16, D1:],
                jnp.where(even, a[lines], b[lines]),
                new[64 * side + 16 * half : 64 * side + 16 * half + 16],
                jnp.where(even, c, d),
            ],
            axis=0,
        )
        keys.append(kv[:, 0:D1])
        values.append(kv[:, D1:])
        queries.append(own_edge_ref[at : at + 16, 0:D1])
        starts = (4, 0) if side == 0 else (COLS, COLS + 4)
        pieces = [
            jnp.broadcast_to(turned[c0 : c0 + 4, r : r + 1], (4, 128))
            for c0 in starts
            for r in range(8 * half, 8 * half + 8)
        ]
        own_ids = jnp.concatenate(pieces[0:4] * 8, axis=0).T[0:1]
        allowed.append(jnp.concatenate(pieces, axis=0) == own_ids)
    scale = LOG2E / math.sqrt(32)
    units = [(w, g) for w in range(4) for g in range(2)]
    scores = [
        lax.dot_general(
            keys[w][:, 256 * g : 256 * g + 256],
            masked_heads(queries[w][:, 256 * g : 256 * g + 256], 32, 8),
            NT,
            preferred_element_type=F32,
        )
        for w, g in units
    ]
    probs = [
        softmax_keys(s * scale + bias_ref[windows[w][0], windows[w][1], g], allowed[w]).astype(BF)
        for s, (w, g) in zip(scores, units)
    ]
    outs = [
        lax.dot_general(p, values[w][:, 256 * g : 256 * g + 256], TN, preferred_element_type=F32)
        for p, (w, g) in zip(probs, units)
    ]
    picked = [pick_heads(o, 32, 8).astype(BF) for o in outs]
    attended = [jnp.concatenate(picked[2 * w : 2 * w + 2], axis=1) for w in range(4)]
    edge = jnp.dot(jnp.concatenate(attended, axis=0), out_ref[...], preferred_element_type=F32)
    for row in range(ROWS):
        half, r = row // 4, row % 4
        at = 32 * half + 4 * r
        adds = [edge[at : at + 4]]
        for j in range(INSIDE):
            tile = slice(32 * j + 8 * r, 32 * j + 8 * r + 8)
            upper, lower = cross_add_ref[tile], pair_add_ref[tile]
            if half == 1:
                upper, lower = lower, upper
            adds.append(jnp.where(even, upper, lower))
        adds.append(edge[at + 16 : at + 20])
        value = (tok_ref[row].astype(F32) + jnp.concatenate(adds, axis=0)).astype(BF)
        done[row] = value
        for n in range(4):
            level[n, row] = value[:, n * 128 : n * 128 + 128].astype(F32)
    store = pltpu.make_async_copy(done, one_out, sem)
    store.start()

    means, factors = [], []
    for i in range(4):
        quartet = [
            jnp.concatenate(
                [level[n, 2 * i + dr, pl.ds(dc, COLS // 2, 2), :] for n in range(4)], axis=1
            )
            for dc in range(2)
            for dr in range(2)
        ]
        for n in range(4):
            parts[n, :, i] = quartet[n].reshape(3, 8, D1)
        mean, factor = row_stats(quartet)
        means.append(mean)
        factors.append(factor)
    order = [(i, slice(8 * w, 8 * w + 8)) for w in range(3) for i in range(4)]
    mean = jnp.concatenate([means[i][at] for i, at in order], axis=0)
    factor = jnp.concatenate([factors[i][at] for i, at in order], axis=0)
    total = jnp.zeros((112, D2), F32)
    for n in range(4):
        total += jnp.dot(
            with_ones(parts[n].reshape(96, D1).astype(BF)),
            merge_ref[n * D1 : (n + 1) * D1, :],
            preferred_element_type=F32,
        )
    merged = after_norm(total, mean, factor).astype(BF)
    merged_out[...] = merged
    mean, factor = row_stats([merged.astype(F32)])
    total = jnp.dot(with_ones(merged), two_ref[:, 512:], preferred_element_type=F32)
    kv_out[...] = after_norm(total, mean, factor).astype(BF)
    store.wait()


TWO_UNITS = [(w, g) for w in range(3) for g in range(2)]


def scores_two(keys_ref, queries, bias):
    scale = LOG2E / math.sqrt(64)
    return [
        lax.dot_general(
            keys_ref[w * 32 : w * 32 + 32, g * 256 : g * 256 + 256],
            masked_heads(queries[w * 32 : w * 32 + 32, g * 256 : g * 256 + 256], 64, 4),
            NT,
            preferred_element_type=F32,
        )
        * scale
        + bias[g]
        for w, g in TWO_UNITS
    ]


def query_kernel(merged_ref, kv_ref, bias_ref, two_ref, query_out, score_out):
    merged = merged_ref[...]
    mean, factor = row_stats([merged.astype(F32)])
    total = jnp.dot(with_ones(merged), two_ref[:, :512], preferred_element_type=F32)
    q = after_norm(total, mean, factor).astype(BF)
    query_out[...] = q
    for n, s in enumerate(scores_two(kv_ref, q, [bias_ref[g, 0:32] for g in range(2)])):
        score_out[n] = s


def level_two_kernel(
    query_ref, score_ref, kv_ref, other_ref, merged_ref, bias_ref, out_ref, two_out, result, sems
):
    far = scores_two(other_ref, query_ref[...], [bias_ref[g, 32:64] for g in range(2)])
    probs = [
        softmax_keys(jnp.concatenate([score_ref[n], s], axis=0), None).astype(BF)
        for n, s in enumerate(far)
    ]
    outs = []
    for p, (w, g) in zip(probs, TWO_UNITS):
        block = (slice(w * 32, w * 32 + 32), slice(512 + g * 256, 768 + g * 256))
        values = jnp.concatenate([kv_ref[block], other_ref[block]], axis=0)
        outs.append(lax.dot_general(p, values, TN, preferred_element_type=F32))
    picked = [pick_heads(o, 64, 4).astype(BF) for o in outs]
    attended = jnp.concatenate(
        [jnp.concatenate(picked[2 * w : 2 * w + 2], axis=1) for w in range(3)], axis=0
    )
    stores = []
    for part in range(2):
        lanes = slice(part * 512, part * 512 + 512)
        y = merged_ref[:, lanes].astype(F32) + jnp.dot(
            attended, out_ref[:, lanes], preferred_element_type=F32
        )
        for i in range(4):
            tiles = [y[32 * w + 8 * i : 32 * w + 8 * i + 8] for w in range(3)]
            result[i, :, lanes] = jnp.concatenate(tiles, axis=0).astype(BF)
        stores.append(
            pltpu.make_async_copy(result.at[:, :, lanes], two_out.at[:, :, lanes], sems.at[part])
        )
        stores[-1].start()
    for store in stores:
        store.wait()


def call(kernel, outs, args, hbm=0, scratch=(), mib=16, us=1.0, hbm_outs=0):
    shapes = [jax.ShapeDtypeStruct(s, d) for s, d in outs]
    place = [pl.BlockSpec(memory_space=pltpu.HBM)] * hbm
    place += [pl.BlockSpec(memory_space=pltpu.VMEM)] * (len(args) - hbm)
    args = [
        pltpu.with_memory_space_constraint(x, pltpu.HBM) if n < hbm else x
        for n, x in enumerate(args)
    ]
    return pl.pallas_call(
        kernel,
        out_shape=shapes,
        in_specs=place,
        out_specs=[pl.BlockSpec(memory_space=pltpu.HBM)] * hbm_outs
        + [pl.BlockSpec(memory_space=pltpu.VMEM)] * (len(outs) - hbm_outs),
        scratch_shapes=list(scratch),
        compiler_params=pltpu.CompilerParams(vmem_limit_bytes=mib * MIB),
        cost_estimate=pl.CostEstimate(
            flops=int(us * 10**9), bytes_accessed=10**6, transcendentals=0
        ),
        name=kernel.__name__,
    )(*args)


def on_device(
    tokens, region_ids, bias_one, qkv_one, out_one, merge_proj, bias_two, qkv_two, out_two
):
    lats, lons = lax.axis_size("lat"), lax.axis_size("lon")
    lat_inner = [(i, i ^ 1) for i in range(lats)]
    lat_outer = [(i, (i + (1 if i % 2 else -1)) % lats) for i in range(lats)]
    lon_inner = [(i, i ^ 1) for i in range(lons)]
    lon_outer = [(i, (i + (1 if i % 2 else -1)) % lons) for i in range(lons)]

    cross, pair, region_ids = call(
        load_kernel,
        [((200, D1), BF), ((200, D1), BF), ((ROWS, COLS), jnp.int32)],
        [tokens, region_ids],
        hbm=2,
        scratch=[pltpu.SemaphoreType.DMA((9,))],
        mib=4,
        us=4.0,
    )
    cross = lax.ppermute(cross, "lat", lat_outer)
    pair = lax.ppermute(pair, "lat", lat_inner)
    inside, own_edge, table_one, table_side, table_two = call(
        own_kernel,
        [
            ((2, INSIDE, 32, 3 * D1), BF), ((64, 3 * D1), BF), ((2, 4, 64, 128), F32),
            ((2, 2, 2, 64, 128), F32), ((2, 64, 128), F32),
        ],
        [qkv_one, bias_one, bias_two, tokens],
        scratch=[pltpu.VMEM((2, INSIDE, 2, 16, D1), BF)],
        us=1.5,
    )
    half_shape = pltpu.VMEM((INSIDE, 2, 16, D1), BF)
    pair_add, pair_edge = call(
        pair_kernel,
        [((INSIDE * 32, D1), F32), ((32, 2 * D1), BF)],
        [pair, region_ids, inside, qkv_one, table_one, out_one],
        scratch=[half_shape],
        us=0.3,
    )
    inner, outer, ids = call(
        edge_kernel,
        [((72, D1), BF), ((72, D1), BF), ((2 * ROWS, 128), F32)],
        [tokens, region_ids, pair, cross, pair_add],
        mib=4,
    )
    inner = lax.ppermute(inner, "lon", lon_inner)
    outer = lax.ppermute(outer, "lon", lon_outer)
    cross_add, cross_edge = call(
        cross_kernel,
        [((INSIDE * 32, D1), F32), ((32, 2 * D1), BF)],
        [cross, ids, inside, qkv_one, table_one, out_one],
        scratch=[half_shape],
        us=0.3,
    )
    level_one, merged, kv = call(
        final_kernel,
        [((ROWS, COLS, D1), BF), ((96, D2), BF), ((96, 1024), BF)],
        [
            tokens, inner, outer, ids, qkv_one, table_side, out_one, own_edge, pair_edge,
            cross_edge, pair_add, cross_add, merge_proj, qkv_two,
        ],
        scratch=[
            pltpu.VMEM((4, ROWS, COLS, 128), F32),
            pltpu.VMEM((4, 3, 4, 8, D1), F32),
            pltpu.VMEM((ROWS, COLS, D1), BF),
            pltpu.SemaphoreType.DMA,
        ],
        hbm_outs=1,
    )
    other_kv = lax.ppermute(kv, "lat", lat_inner)
    query, scores = call(
        query_kernel,
        [((96, 512), BF), ((6, 32, 128), F32)],
        [merged, kv, table_two, qkv_two],
    )
    (level_two,) = call(
        level_two_kernel,
        [((4, 24, D2), BF)],
        [query, scores, kv, other_kv, merged, table_two, out_two],
        scratch=[pltpu.VMEM((4, 24, D2), BF), pltpu.SemaphoreType.DMA((2,))],
        hbm_outs=1,
    )
    return (level_one, level_two)


def solution(mesh):
    placed = (P("lat", "lon", None), P("lat", "lon"), P(), P(), P(), P(), P(), P(), P())
    return jax.shard_map(
        on_device,
        mesh=mesh,
        in_specs=placed,
        out_specs=(P("lat", "lon", None), P("lat", "lon", None)),
        check_vma=False,
    )
```
